32 devices in a mesh: kv: 2 (over core), seq: 16 (over z, y, x).
Axes of the slice: x: 2, y: 2, z: 4, core: 2. Of those that a mesh axis runs over, the one named last changes fastest.
Arguments:
- tokens: bfloat16 [4096, 4096], P(('seq', 'kv')), may hold values from -6 to 6
- gain: float32 [4096], replicated, may hold values from 0.25 to 1.75
- w_query: bfloat16 [4096, 4096], P(None, 'kv'), may hold values from -1 to 1
- w_key: bfloat16 [4096, 1024], P(None, 'kv'), may hold values from -4 to 4
- w_value: bfloat16 [4096, 1024], P(None, 'kv'), may hold values from -0.09375 to 0.09375
- w_out: bfloat16 [4096, 4096], P('kv'), may hold values from -0.09375 to 0.09375
- segment_ids: int32 [4096], replicated, may hold values from 0 to 4095, as said below
- page_table: int32 [32], P('seq'), may hold values from 0 to 1, as said below
Outputs:
- mixed: bfloat16 [4096, 4096], P(('seq', 'kv'))
- attn_out: bfloat16 [4096, 4096], P(('seq', 'kv'))
- page_pool: bfloat16 [32, 2, 8, 128, 128], P('seq', None, 'kv')
The draws below stay inside these ranges and needn't reach their ends.
Inputs may be any that keep to these rules, and one draw needn't show every extreme that they name: `segment_ids`: never falls along the stream; tokens of one prompt share the position of its first token as id; every prompt has 1 to 1792 tokens; exactly two prompts have 1792 tokens, one in each half of the stream, each beginning inside a block of 256 tokens and not at its first token; every other prompt has fewer than 128 tokens; the last token of the stream is a prompt of its own. `page_table`: in each aligned block of 2 entries every value appears once.
All inputs are finite; a program needn't handle non-finite values.
Results may differ from the reference program's by a relative error of at most 0.0065.
The reference program's roundings to bfloat16 on the way (of `normed`, `query`, `key_rows`, `value_rows`, `weights` and `attention`) count: a program that leaves them out, or rounds other values in their place, can miss the bound.
Values may be sent and summed in bfloat16 or wider, within the bound.
No kernel may reach another device: no remote copies, remote signals or barrier semaphores. Data moves between devices by JAX's collectives and lax.ppermute only.
A program may use at most 192 MiB of HBM per device.

```python
import jax
import jax.numpy as jnp
from jax import lax

D = 4096
HEADS = 32
KVH = 8
HD = 128
PAGE = 128
SHORT = 64
BLOCK = 256
TOKENS = 4096
REACH = 7
LONGSEG = 1792
PAGES = 32
PAGES_DEV = 2
N_SEQ = 16


def draw_tokens(key, part):
    key_base = jax.random.fold_in(key, 0)
    base_draw = jax.random.normal(key_base, (TOKENS, D), jnp.float32)
    return jnp.clip(base_draw, -6.0, 6.0).astype(jnp.bfloat16)


def shared_query(key):
    return jax.random.normal(jax.random.fold_in(key, 11), (D, HEADS * HD), jnp.float32) * D ** (-0.5)


def draw_w_query(key, part):
    return jnp.clip(shared_query(key), -1.0, 1.0).astype(jnp.bfloat16)


def draw_w_key(key, part):
    result = jax.random.normal(jax.random.fold_in(key, 12), (D, KVH * HD), jnp.float32) * D ** (-0.5)
    return jnp.clip(result, -4.0, 4.0).astype(jnp.bfloat16)


def draw_segment_ids(key, part):
    key_lengths, key_block_one, key_block_two, key_offset_one, key_offset_two = jax.random.split(key, 5)
    position = jnp.arange(TOKENS, dtype=jnp.int32)
    lengths = jax.random.randint(key_lengths, (TOKENS,), 1, 2 * SHORT, dtype=jnp.int32)
    starts = jnp.cumsum(lengths) - lengths
    flags = jnp.zeros((TOKENS,), jnp.int32).at[starts].set(1, mode='drop')
    half_blocks = TOKENS // BLOCK // 2
    block_keys = (key_block_one, key_block_two)
    offset_keys = (key_offset_one, key_offset_two)
    for which in range(2):
        first_block = jax.random.randint(block_keys[which], (), 0, half_blocks - REACH, dtype=jnp.int32) + which * half_blocks
        begin = first_block * BLOCK + jax.random.randint(offset_keys[which], (), 1, BLOCK, dtype=jnp.int32)
        inside = (position >= begin) & (position < begin + LONGSEG)
        flags = jnp.where(inside, 0, flags)
        flags = jnp.where((position == begin) | (position == begin + LONGSEG), 1, flags)
    flags = flags.at[0].set(1)
    flags = flags.at[TOKENS - 1].set(1)
    marked = jnp.where(flags > 0, position, 0)
    return lax.cummax(marked, axis=0).astype(jnp.int32)


def draw_page_table(key, part):
    block_keys = jax.random.split(key, PAGES // PAGES_DEV)
    orders = jax.vmap(lambda single: jax.random.permutation(single, PAGES_DEV))(block_keys)
    return orders.reshape(PAGES).astype(jnp.int32)


def block_levels(key, extent, shards, least, top_value):
    loudness, own = 1.0, jax.random.fold_in(key, 6)
    for dim, shards_of in shards:
        steps = jnp.exp(jax.random.uniform(jax.random.fold_in(own, dim), (shards_of,), jnp.float32, least / len(shards), top_value / len(shards)))
        loudness = loudness * jnp.repeat(steps, extent[dim] // shards_of).reshape([-1 if axis == dim else 1 for axis in range(len(extent))])
    return loudness


def normal_values(key, dims, width, most, cuts=(), kind=jnp.bfloat16):
    level = block_levels(key, dims, cuts, -0.22, 0.18) if cuts else 1.0
    entries = jax.random.normal(key, dims, jnp.float32) * width * level
    return jnp.minimum(jnp.maximum(entries, -most), most).astype(kind)


def setup_inputs(seed: int = 0) -> dict:
    seeds = jax.random.split(jax.random.key(seed), 9)
    return {
        "tokens": draw_tokens(jax.random.fold_in(seeds[8], 71), 0),
        "gain": jnp.clip(1.0 + 0.15 * jax.random.normal(seeds[1], (D,), jnp.float32), 0.25, 1.75),
        "w_query": draw_w_query(jax.random.fold_in(seeds[8], 71), 0),
        "w_key": draw_w_key(jax.random.fold_in(seeds[8], 71), 0),
        "w_value": normal_values(seeds[4], (D, KVH * HD), D ** -0.5, 0.09375, ((1, 2),)),
        "w_out": normal_values(seeds[5], (HEADS * HD, D), (HEADS * HD) ** -0.5, 0.09375, ((0, 2),)),
        "segment_ids": draw_segment_ids(jax.random.fold_in(seeds[8], 71), 0),
        "page_table": draw_page_table(jax.random.fold_in(seeds[8], 71), 0),
    }


norm_eps = 1e-05

def head_attention(query_head, key_blocks, value_blocks, masks, live):
    block_count = key_blocks.shape[0]
    key_width = key_blocks.shape[1]
    score_scale = query_head.shape[-1] ** (-0.5)
    query_wide = query_head.astype(jnp.float32)

    def block_scores(distance):
        scores = jnp.einsum('qgd,kd->gqk', query_wide, key_blocks[distance].astype(jnp.float32)) * score_scale
        return jnp.where(masks[distance][None], scores, -jnp.inf)

    def empty_scores():
        return jnp.full((query_head.shape[1], query_head.shape[0], key_width), -jnp.inf, jnp.float32)
    pieces = [block_scores(0)]
    for distance in range(1, block_count):
        pieces.append(lax.cond(live[distance], lambda: block_scores(distance), empty_scores))
    scores = jnp.concatenate(pieces, axis=2)
    row_peak = lax.optimization_barrier(jnp.max(scores, axis=2, keepdims=True))
    weights = jnp.exp(scores - row_peak).astype(jnp.bfloat16)
    weights_wide = weights.astype(jnp.float32)
    row_total = lax.optimization_barrier(jnp.sum(weights_wide, axis=2))
    all_values = value_blocks.reshape(block_count * key_width, value_blocks.shape[-1]).astype(jnp.float32)
    weighted = jnp.einsum('gqk,kd->qgd', weights_wide, all_values)
    return (weighted / row_total.T[:, :, None]).astype(jnp.bfloat16)

def reference(tokens, gain, w_query, w_key, w_value, w_out, segment_ids, page_table):
    wide_rows = tokens.astype(jnp.float32)
    normed = (wide_rows * lax.rsqrt(lax.optimization_barrier(jnp.mean(wide_rows * wide_rows, axis=1, keepdims=True)) + norm_eps) * gain).astype(jnp.bfloat16)
    query = jnp.dot(normed, w_query, preferred_element_type=jnp.float32).astype(jnp.bfloat16)
    key_rows = jnp.dot(normed, w_key, preferred_element_type=jnp.float32).astype(jnp.bfloat16)
    value_rows = jnp.dot(normed, w_value, preferred_element_type=jnp.float32).astype(jnp.bfloat16)
    pair_rows = jnp.stack([key_rows, value_rows], axis=0)
    pages = pair_rows.reshape(2, PAGES, PAGE, KVH, HD).transpose(1, 0, 3, 2, 4)
    slots = jnp.arange(PAGES, dtype=jnp.int32) // PAGES_DEV * PAGES_DEV + page_table.astype(jnp.int32)
    page_pool = jnp.zeros_like(pages).at[slots].set(pages)
    group_size = HEADS // KVH
    query_blocks = query.reshape(N_SEQ, BLOCK, KVH, group_size, HD)
    key_blocks = key_rows.reshape(N_SEQ, BLOCK, KVH, HD)
    value_blocks = value_rows.reshape(N_SEQ, BLOCK, KVH, HD)
    lower = jnp.arange(BLOCK)[None, :] <= jnp.arange(BLOCK)[:, None]

    def one_block(index):
        query_here = query_blocks[index]
        query_segs = lax.dynamic_slice_in_dim(segment_ids, (index * BLOCK).astype(jnp.int32), BLOCK)
        key_list, value_list, mask_list, live_list = ([], [], [], [])
        for distance in range(REACH + 1):
            source = jnp.maximum(index - distance, 0).astype(jnp.int32)
            valid = index - distance >= 0
            key_list.append(key_blocks[source])
            value_list.append(value_blocks[source])
            key_segs = lax.dynamic_slice_in_dim(segment_ids, (source * BLOCK).astype(jnp.int32), BLOCK)
            same = (key_segs[None, :] == query_segs[:, None]) & valid
            if distance == 0:
                same = same & lower
                live_list.append(jnp.array(True))
            else:
                live_list.append(valid & (key_segs[BLOCK - 1] == query_segs[0]))
            mask_list.append(same)
        masks = jnp.stack(mask_list)
        live = jnp.stack(live_list)
        keys_all = jnp.stack(key_list).transpose(2, 0, 1, 3)
        values_all = jnp.stack(value_list).transpose(2, 0, 1, 3)

        def per_head(inputs):
            return head_attention(inputs[0], inputs[1], inputs[2], masks, live)
        heads_out = lax.map(per_head, (query_here.transpose(1, 0, 2, 3), keys_all, values_all))
        return heads_out.transpose(1, 0, 2, 3).reshape(BLOCK, HEADS * HD)
    attention = lax.map(one_block, jnp.arange(N_SEQ, dtype=jnp.int32)).reshape(TOKENS, HEADS * HD)
    branch = jnp.dot(attention, w_out, preferred_element_type=jnp.float32)
    attn_out = branch.astype(jnp.bfloat16)
    mixed = (wide_rows + branch).astype(jnp.bfloat16)
    return (mixed, attn_out, page_pool)
```

```python
import functools
import math

import jax
import jax.numpy as jnp
from jax import lax
from jax.experimental import pallas as pl
from jax.experimental.pallas import tpu as pltpu
from jax.sharding import PartitionSpec as P

HD = 128
NORM_EPS = 1e-05
MASKED = -1e30
MIB = 1024 * 1024


def project_kv_kernel(own_ref, other_ref, gain_ref, wk_ref, wv_ref, normed_ref, kv_ref):
    half = own_ref.shape[0]

    @pl.when(pl.program_id(0) == 0)
    def _():
        for index, ref in enumerate((own_ref, other_ref)):
            for start in range(0, half, 32):
                wide = ref[start : start + 32, :].astype(jnp.float32)
                mean = jnp.mean(wide * wide, axis=1, keepdims=True)
                normed = wide * lax.rsqrt(mean + NORM_EPS) * gain_ref[...]
                first = index * half + start
                normed_ref[first : first + 32, :] = normed.astype(jnp.bfloat16)

    weights = jnp.concatenate([wk_ref[...], wv_ref[...]], axis=1)
    pair = jnp.dot(normed_ref[...], weights, preferred_element_type=jnp.float32)
    pair = pair.astype(jnp.bfloat16)
    kv_ref[0, 0] = pair[:, :HD]
    kv_ref[0, 1] = pair[:, HD:]


def project_kv(own, other, gain, w_key, w_value):
    half, width = own.shape
    heads = w_key.shape[1] // HD
    rows = 2 * half
    whole = lambda h: (0, 0)
    return pl.pallas_call(
        project_kv_kernel,
        grid=(heads,),
        in_specs=[
            pl.BlockSpec((half, width), whole),
            pl.BlockSpec((half, width), whole),
            pl.BlockSpec((1, width), whole),
            pl.BlockSpec((width, HD), lambda h: (0, h)),
            pl.BlockSpec((width, HD), lambda h: (0, h)),
        ],
        out_specs=[
            pl.BlockSpec((rows, width), whole),
            pl.BlockSpec((1, 2, rows, HD), lambda h: (h, 0, 0, 0)),
        ],
        out_shape=[
            jax.ShapeDtypeStruct((rows, width), jnp.bfloat16),
            jax.ShapeDtypeStruct((heads, 2, rows, HD), jnp.bfloat16),
        ],
        compiler_params=pltpu.CompilerParams(vmem_limit_bytes=32 * MIB),
        cost_estimate=pl.CostEstimate(
            flops=4 * rows * width * heads * HD,
            bytes_accessed=4 * width * heads * HD + 4 * rows * width,
            transcendentals=0,
        ),
        name="project_kv",
    )(own, other, gain.reshape(1, width), w_key, w_value)


def matmul_kernel(x_ref, w_ref, out_ref):
    out_ref[...] = jnp.dot(x_ref[...], w_ref[...], preferred_element_type=jnp.float32).astype(
        out_ref.dtype
    )


def project_query(normed, w_query, tile=256):
    rows, width = normed.shape
    cols = w_query.shape[1]
    return pl.pallas_call(
        matmul_kernel,
        grid=(cols // tile,),
        in_specs=[
            pl.BlockSpec((rows, width), lambda n: (0, 0)),
            pl.BlockSpec((width, tile), lambda n: (0, n)),
        ],
        out_specs=pl.BlockSpec((rows, tile), lambda n: (0, n)),
        out_shape=jax.ShapeDtypeStruct((rows, cols), jnp.bfloat16),
        compiler_params=pltpu.CompilerParams(vmem_limit_bytes=32 * MIB),
        cost_estimate=pl.CostEstimate(
            flops=2 * rows * width * cols,
            bytes_accessed=2 * (width * cols + rows * (width + cols)),
            transcendentals=0,
        ),
        name="project_query",
    )(normed, w_query)


def attention_kernel(block_count, first, last, group, *refs):
    seg_q, pos_q, seg_k, pos_k, q_ref = refs[:5]
    blocks = refs[5 : 5 + block_count]
    refs = refs[5 + block_count :]
    if not first:
        acc_in, stat_in = refs[:2]
        refs = refs[2:]
    if last:
        out_ref, bias_ref = refs
    else:
        acc_out, stat_out, bias_ref = refs

    @pl.when(pl.program_id(0) == 0)
    def _():
        seen = (seg_q[...] == seg_k[...]) & (pos_k[...] <= pos_q[...])
        bias_ref[...] = jnp.where(seen, 0.0, MASKED)

    rows = q_ref.shape[0]
    factor = math.log2(math.e) / math.sqrt(HD)
    keys = jnp.concatenate([block[0, 0] for block in blocks], axis=0)
    values = jnp.concatenate([block[0, 1] for block in blocks], axis=0)
    values = jnp.concatenate([values, jnp.ones_like(values)], axis=1)
    for head in range(group):
        cols = slice(head * HD, (head + 1) * HD)
        scores = lax.dot_general(
            q_ref[:, cols], keys, (((1,), (1,)), ((), ())), preferred_element_type=jnp.float32
        )
        scores = scores + bias_ref[...]
        peak = jnp.max(scores, axis=1, keepdims=True)
        if not first:
            old = stat_in[0, :, head : head + 1]
            peak = jnp.maximum(peak, old)
        weights = jnp.exp2(scores * factor - peak * factor).astype(jnp.bfloat16)
        total = jnp.dot(weights, values, preferred_element_type=jnp.float32)
        acc = total[:, :HD]
        mass = total[:, HD:]
        if not first:
            keep = jnp.exp2((old - peak) * factor)
            acc = acc + acc_in[:, cols] * keep
            mass = mass + stat_in[0, :, group + head : group + head + 1] * keep
        if last:
            out_ref[:, cols] = (acc / mass).astype(jnp.bfloat16)
        else:
            acc_out[:, cols] = acc
            stat_out[0, :, head : head + 1] = peak
            stat_out[0, :, group + head : group + head + 1] = mass[:, :1]


def attend(query, blocks, sources, segs, positions, state, last):
    rows, q_cols = query.shape
    heads = blocks[0].shape[0]
    width = q_cols // heads
    group = width // HD
    seg_of, pos_of = segs, positions
    seg_k = jnp.concatenate([seg_of(s) for s in sources])[None, :]
    pos_k = jnp.concatenate([pos_of(s) for s in sources])[None, :]
    seg_q = seg_of(None)[:, None]
    pos_q = pos_of(None)[:, None]
    keys = len(blocks) * rows
    first = state is None
    whole = lambda h: (0, 0)
    acc_spec = pl.BlockSpec((rows, width), lambda h: (0, h))
    stat_spec = pl.BlockSpec((1, rows, HD), lambda h: (h, 0, 0))
    in_specs = [
        pl.BlockSpec((rows, 1), whole),
        pl.BlockSpec((rows, 1), whole),
        pl.BlockSpec((1, keys), whole),
        pl.BlockSpec((1, keys), whole),
        pl.BlockSpec((rows, width), lambda h: (0, h)),
    ]
    in_specs += [pl.BlockSpec((1, 2, rows, HD), lambda h: (h, 0, 0, 0))] * len(blocks)
    if not first:
        in_specs += [acc_spec, stat_spec]
    if last:
        out_specs = acc_spec
        out_shape = jax.ShapeDtypeStruct((rows, q_cols), jnp.bfloat16)
    else:
        out_specs = [acc_spec, stat_spec]
        out_shape = [
            jax.ShapeDtypeStruct((rows, q_cols), jnp.float32),
            jax.ShapeDtypeStruct((heads, rows, HD), jnp.float32),
        ]
    return pl.pallas_call(
        functools.partial(attention_kernel, len(blocks), first, last, group),
        grid=(heads,),
        in_specs=in_specs,
        out_specs=out_specs,
        out_shape=out_shape,
        scratch_shapes=[pltpu.VMEM((rows, keys), jnp.float32)],
        compiler_params=pltpu.CompilerParams(vmem_limit_bytes=48 * MIB),
        cost_estimate=pl.CostEstimate(
            flops=6 * rows * keys * q_cols,
            bytes_accessed=8 * rows * q_cols,
            transcendentals=rows * keys * heads * group,
        ),
        name="attend",
    )(seg_q, pos_q, seg_k, pos_k, query, *blocks, *(state or ()))


def project_out_kernel(x_ref, w_ref, own_ref, other_ref):
    half = own_ref.shape[0]
    part = jnp.dot(x_ref[...], w_ref[...], preferred_element_type=jnp.float32)
    own_ref[...] = part[:half]
    other_ref[...] = part[half:].astype(other_ref.dtype)


def project_out(attention, w_out, piece, pieces, tile=256):
    rows, depth = attention.shape
    cols = w_out.shape[1] // pieces
    tiles = cols // tile
    half = rows // 2
    return pl.pallas_call(
        project_out_kernel,
        grid=(tiles,),
        in_specs=[
            pl.BlockSpec((rows, depth), lambda n: (0, 0)),
            pl.BlockSpec((depth, tile), lambda n: (0, piece * tiles + n)),
        ],
        out_specs=[
            pl.BlockSpec((half, tile), lambda n: (0, n)),
            pl.BlockSpec((half, tile), lambda n: (0, n)),
        ],
        out_shape=[
            jax.ShapeDtypeStruct((half, cols), jnp.float32),
            jax.ShapeDtypeStruct((half, cols), jnp.bfloat16),
        ],
        compiler_params=pltpu.CompilerParams(vmem_limit_bytes=32 * MIB),
        cost_estimate=pl.CostEstimate(
            flops=2 * rows * depth * cols,
            bytes_accessed=2 * depth * cols + 6 * half * cols,
            transcendentals=0,
        ),
        name="project_out",
    )(attention, w_out)


def swap_cores(value):
    return lax.ppermute(value, "kv", [(0, 1), (1, 0)])


def gather_in_half(block, index, count):
    half = count // 2

    def exchange(value, bit):
        return lax.ppermute(value, "seq", [(i, i ^ bit) for i in range(count)])

    pairs = [(i, i ^ 4) for i in range(count)]
    for start in range(half, count, half):
        before = start - 1
        pairs = [p for p in pairs if p[0] != before and p[1] != start] + [(before, start)]
    from_x = exchange(block, 1)
    from_y = exchange(block, 2)
    from_z = lax.ppermute(block, "seq", pairs)
    seam = (index % half == 0) & (index > 0)
    z_source = jnp.where(seam, index - 1, index ^ 4)
    near = [(from_x, index ^ 1), (from_y, index ^ 2), (from_z, z_source)]
    from_xy = exchange(from_y, 1)
    from_yz = exchange(from_z, 2)
    from_xz = exchange(from_x, 4)
    far = [(from_xy, index ^ 3), (from_yz, index ^ 6), (from_xz, index ^ 5)]
    flat = lambda value: value.reshape((-1,) + value.shape[2:])
    last = jnp.concatenate(
        [
            exchange(flat(from_yz)[:3], 1),
            exchange(flat(from_xz)[3:6], 2),
            exchange(flat(from_xy)[6:], 4),
        ]
    ).reshape(block.shape)
    return [near, far, [(last, index ^ 7)]]


def gather_by_distance(block, index, count, reach):
    received = []
    for distance in range(1, reach + 1):
        moved = lax.ppermute(block, "seq", [(i, i + distance) for i in range(count - distance)])
        received.append((moved, index - distance))
    return [received[start : start + 3] for start in range(0, reach, 3)]


def shards(tokens, gain, w_query, w_key, w_value, w_out, segment_ids, page_table):
    half_rows = tokens.shape[0]
    block_rows = 2 * half_rows
    count = lax.axis_size("seq")
    index = lax.axis_index("seq")
    core = lax.axis_index("kv")
    reach = min(8, count // 2 - 1)

    other_tokens = swap_cores(tokens)
    normed, own_block = project_kv(tokens, other_tokens, gain, w_key, w_value)

    if count == 2 * (reach + 1) and count // 2 == 8:
        groups = gather_in_half(own_block, index, count)
    else:
        groups = gather_by_distance(own_block, index, count, reach)

    query = project_query(normed, w_query)

    offsets = jnp.arange(half_rows, dtype=jnp.int32)
    local = jnp.concatenate([core * half_rows + offsets, (1 - core) * half_rows + offsets])

    def positions(source):
        return (index if source is None else source) * block_rows + local

    def segs(source):
        start = jnp.maximum(index if source is None else source, 0) * block_rows
        first = lax.dynamic_slice_in_dim(segment_ids, start + core * half_rows, half_rows)
        second = lax.dynamic_slice_in_dim(segment_ids, start + (1 - core) * half_rows, half_rows)
        found = jnp.concatenate([first, second])
        return found if source is None else jnp.where(source >= 0, found, -1)

    groups[0] = [(own_block, index)] + groups[0]
    state = None
    for number, group in enumerate(groups):
        blocks = [block for block, _ in group]
        sources = [source for _, source in group]
        state = attend(
            query, blocks, sources, segs, positions, state, number == len(groups) - 1
        )
    attention = state

    heads = own_block.shape[0]
    pages = own_block.reshape(heads, 2, 2, half_rows, HD).transpose(2, 1, 0, 3, 4)
    own_slot = lax.dynamic_index_in_dim(page_table, core, keepdims=False)
    page_pool = jnp.where(own_slot == 0, pages, pages[::-1])

    pieces = 2
    wide = tokens.astype(jnp.float32)
    cols = w_out.shape[1] // pieces
    attn_out, mixed = [], []
    parts = [project_out(attention, w_out, piece, pieces) for piece in range(pieces)]
    for piece, (mine, theirs) in enumerate(parts):
        branch = mine + swap_cores(theirs).astype(jnp.float32)
        attn_out.append(branch.astype(jnp.bfloat16))
        mixed.append(
            (wide[:, piece * cols : (piece + 1) * cols] + branch).astype(jnp.bfloat16)
        )
    return (jnp.concatenate(mixed, axis=1), jnp.concatenate(attn_out, axis=1), page_pool)


def solution(mesh):
    in_specs = (
        P(("seq", "kv"), None),
        P(),
        P(None, "kv"),
        P(None, "kv"),
        P(None, "kv"),
        P("kv", None),
        P(),
        P("seq"),
    )
    out_specs = (P(("seq", "kv"), None), P(("seq", "kv"), None), P("seq", None, "kv", None, None))
    return jax.shard_map(shards, mesh=mesh, in_specs=in_specs, out_specs=out_specs, check_vma=False)
```

```python
import functools
import math

import jax
import jax.numpy as jnp
from jax import lax
from jax.experimental import pallas as pl
from jax.experimental.pallas import tpu as pltpu
from jax.sharding import PartitionSpec as P

HD = 128
NORM_EPS = 1e-05
MASKED = -1e30
MIB = 1024 * 1024


IN_VMEM = pl.BlockSpec(memory_space=pltpu.VMEM)
IN_PLACE = pl.BlockSpec(memory_space=pl.ANY)


def call(kernel, name, args, outs, flops, limit=8, scratch=(), out_specs=IN_VMEM, exps=0):
    outs_list = outs if isinstance(outs, list) else [outs]
    moved = sum(math.prod(a.shape) * a.dtype.itemsize for a in list(args) + outs_list)
    return pl.pallas_call(
        kernel,
        in_specs=[IN_VMEM] * len(args),
        out_specs=jax.tree.map(lambda _: out_specs, outs),
        out_shape=outs,
        scratch_shapes=scratch,
        compiler_params=pltpu.CompilerParams(vmem_limit_bytes=limit * MIB),
        cost_estimate=pl.CostEstimate(flops=flops, bytes_accessed=moved, transcendentals=exps),
        name=name,
    )(*args)


def norm_kernel(x_ref, gain_ref, out_ref):
    step = 16
    for start in range(0, x_ref.shape[0], step):
        wide = x_ref[start : start + step, :].astype(jnp.float32)
        mean = jnp.mean(wide * wide, axis=1, keepdims=True)
        normed = wide * lax.rsqrt(mean + NORM_EPS) * gain_ref[...]
        out_ref[start : start + step, :] = normed.astype(jnp.bfloat16)


def norm(tokens, gain):
    out = jax.ShapeDtypeStruct(tokens.shape, jnp.bfloat16)
    return call(norm_kernel, "norm", (tokens, gain[None, :]), out, 4 * tokens.size)


def project_kv_kernel(own_ref, other_ref, wk_ref, wv_ref, kv_ref):
    rows = jnp.concatenate([own_ref[...], other_ref[...]], axis=0)
    for head in range(kv_ref.shape[0]):
        cols = slice(head * HD, (head + 1) * HD)
        weights = jnp.concatenate([wk_ref[:, cols], wv_ref[:, cols]], axis=1)
        pair = jnp.dot(rows, weights, preferred_element_type=jnp.float32).astype(jnp.bfloat16)
        kv_ref[head, 0] = pair[:, :HD]
        kv_ref[head, 1] = pair[:, HD:]


def project_kv(own, other, w_key, w_value):
    half, width = own.shape
    heads = w_key.shape[1] // HD
    out = jax.ShapeDtypeStruct((heads, 2, 2 * half, HD), jnp.bfloat16)
    flops = 8 * half * width * heads * HD
    return call(project_kv_kernel, "project_kv", (own, other, w_key, w_value), out, flops)


def project_query_kernel(own_ref, other_ref, w_ref, out_ref):
    rows = jnp.concatenate([own_ref[...], other_ref[...]], axis=0)
    tile = 512
    for start in range(0, w_ref.shape[1], tile):
        part = jnp.dot(
            rows, w_ref[:, start : start + tile], preferred_element_type=jnp.float32
        )
        out_ref[:, start : start + tile] = part.astype(out_ref.dtype)


def project_query(own, other, w_query):
    half, width = own.shape
    out = jax.ShapeDtypeStruct((2 * half, w_query.shape[1]), jnp.bfloat16)
    flops = 4 * half * w_query.size
    return call(project_query_kernel, "project_query", (own, other, w_query), out, flops)


def attention_kernel(block_count, first, last, group, *refs):
    seg_q, pos_q, seg_k, pos_k, q_ref = refs[:5]
    blocks = refs[5 : 5 + block_count]
    refs = refs[5 + block_count :]
    if not first:
        acc_in, peak_in, mass_in = refs[:3]
        refs = refs[3:]
    if last:
        out_ref, bias_ref = refs
    else:
        acc_out, peak_out, mass_out, bias_ref = refs
    seen = (seg_q[...] == seg_k[...]) & (pos_k[...] <= pos_q[...])
    bias_ref[...] = jnp.where(seen, 0.0, MASKED)
    rows = q_ref.shape[0]
    width = seg_k.shape[1]
    factor = math.log2(math.e) / math.sqrt(HD)
    for head in range(q_ref.shape[1] // HD):
        if head % group == 0:
            keys = jnp.concatenate([block[head // group, 0] for block in blocks], axis=0)
            values = jnp.concatenate([block[head // group, 1] for block in blocks], axis=0)
            values = jnp.concatenate([values, jnp.ones_like(values)], axis=1)
        cols = slice(head * HD, (head + 1) * HD)
        scores = lax.dot_general(
            q_ref[:, cols], keys, (((1,), (1,)), ((), ())), preferred_element_type=jnp.float32
        )
        scores = scores + bias_ref[...]
        peak = jnp.broadcast_to(jnp.max(scores, axis=1, keepdims=True), (rows, HD))
        if not first:
            old = peak_in[:, cols]
            peak = jnp.maximum(peak, old)
        shift = peak * factor
        weights = jnp.concatenate(
            [
                jnp.exp2(scores[:, at : at + HD] * factor - shift).astype(jnp.bfloat16)
                for at in range(0, width, HD)
            ],
            axis=1,
        )
        total = jnp.dot(weights, values, preferred_element_type=jnp.float32)
        acc = total[:, :HD]
        mass = total[:, HD:]
        if not first:
            keep = jnp.exp2((old - peak) * factor)
            acc = acc + acc_in[:, cols] * keep
            mass = mass + mass_in[:, cols] * keep
        if last:
            out_ref[:, cols] = (acc / mass).astype(jnp.bfloat16)
        else:
            acc_out[:, cols] = acc
            peak_out[:, cols] = peak
            mass_out[:, cols] = mass


def attend(query, blocks, sources, segs, positions, state, last):
    rows, q_cols = query.shape
    group = q_cols // HD // blocks[0].shape[0]
    seg_k = jnp.concatenate([segs(s) for s in sources])[None, :]
    pos_k = jnp.concatenate([positions(s) for s in sources])[None, :]
    keys = len(blocks) * rows
    args = [segs(None)[:, None], positions(None)[:, None], seg_k, pos_k, query, *blocks]
    first = state is None
    args += [] if first else state
    if last:
        outs = jax.ShapeDtypeStruct((rows, q_cols), jnp.bfloat16)
    else:
        outs = [jax.ShapeDtypeStruct((rows, q_cols), jnp.float32)] * 3
    return call(
        functools.partial(attention_kernel, len(blocks), first, last, group),
        "attend",
        args,
        outs,
        6 * rows * keys * q_cols,
        limit=14,
        scratch=[pltpu.VMEM((rows, keys), jnp.float32)],
        exps=rows * keys * q_cols // HD,
    )


def project_out_kernel(pieces, x_ref, w_ref, own_ref, other_ref, *, piece):
    half = own_ref.shape[0]
    cols = own_ref.shape[1]
    tile = 512
    for start in range(0, cols, tile):
        at = piece * cols + start
        part = jnp.dot(
            x_ref[...], w_ref[:, at : at + tile], preferred_element_type=jnp.float32
        )
        own_ref[:, start : start + tile] = part[:half]
        other_ref[:, start : start + tile] = part[half:].astype(other_ref.dtype)


def project_out(attention, w_out, piece, pieces):
    rows, depth = attention.shape
    cols = w_out.shape[1] // pieces
    outs = [
        jax.ShapeDtypeStruct((rows // 2, cols), jnp.float32),
        jax.ShapeDtypeStruct((rows // 2, cols), jnp.bfloat16),
    ]
    return call(
        functools.partial(project_out_kernel, pieces, piece=piece),
        "project_out",
        (attention, w_out),
        outs,
        2 * rows * depth * cols,
    )


def finish_kernel(pieces, tokens_ref, *refs):
    mine, theirs = refs[:pieces], refs[pieces : 2 * pieces]
    mixed_hbm, out_hbm, mixed, out, sems = refs[2 * pieces :]
    cols = mine[0].shape[1]
    copies = []
    for piece in range(pieces):
        at = slice(piece * cols, (piece + 1) * cols)
        branch = mine[piece][...] + theirs[piece][...].astype(jnp.float32)
        out[:, at] = branch.astype(out.dtype)
        mixed[:, at] = (tokens_ref[:, at].astype(jnp.float32) + branch).astype(mixed.dtype)
        for number, (here, there) in enumerate(((out, out_hbm), (mixed, mixed_hbm))):
            copies.append(
                pltpu.make_async_copy(here.at[:, at], there.at[:, at], sems.at[piece, number])
            )
            copies[-1].start()
    for copy in copies:
        copy.wait()


def finish(tokens, mine, theirs):
    pieces = len(mine)
    outs = [jax.ShapeDtypeStruct(tokens.shape, jnp.bfloat16)] * 2
    return call(
        functools.partial(finish_kernel, pieces),
        "finish",
        (tokens, *mine, *theirs),
        outs,
        2 * tokens.size,
        scratch=[
            pltpu.VMEM(tokens.shape, jnp.bfloat16),
            pltpu.VMEM(tokens.shape, jnp.bfloat16),
            pltpu.SemaphoreType.DMA((pieces, 2)),
        ],
        out_specs=IN_PLACE,
    )


def after(values, *others):
    return lax.optimization_barrier((values, others))[0]


def swap_cores(value):
    return lax.ppermute(value, "kv", [(0, 1), (1, 0)])


def cube_exchanges(block, index, count):
    half = count // 2

    def exchange(value, bit):
        return lax.ppermute(value, "seq", [(i, i ^ bit) for i in range(count)])

    pairs = [(i, i ^ 4) for i in range(count)]
    for start in range(half, count, half):
        before = start - 1
        pairs = [p for p in pairs if p[0] != before and p[1] != start] + [(before, start)]
    from_x = exchange(block, 1)
    from_y = exchange(block, 2)
    from_z = lax.ppermute(block, "seq", pairs)
    seam = (index % half == 0) & (index > 0)
    z_source = jnp.where(seam, index - 1, index ^ 4)
    near = [(from_x, index ^ 1), (from_y, index ^ 2), (from_z, z_source)]
    work = yield near
    from_x, from_y, from_z = after((from_x, from_y, from_z), work)
    from_xy = exchange(from_y, 1)
    from_yz = exchange(from_z, 2)
    from_xz = exchange(from_x, 4)
    far = [(from_xy, index ^ 3), (from_yz, index ^ 6), (from_xz, index ^ 5)]
    work = yield far
    from_xy, from_yz, from_xz = after((from_xy, from_yz, from_xz), work)
    flat = lambda value: value.reshape((-1,) + value.shape[2:])
    last = jnp.concatenate(
        [
            exchange(flat(from_yz)[:3], 1),
            exchange(flat(from_xz)[3:6], 2),
            exchange(flat(from_xy)[6:], 4),
        ]
    ).reshape(block.shape)
    yield [(last, index ^ 7)]


def distance_exchanges(block, index, count, reach):
    step = 3
    for start in range(1, reach + 1, step):
        received = []
        for distance in range(start, min(start + step, reach + 1)):
            moved = lax.ppermute(block, "seq", [(i, i + distance) for i in range(count - distance)])
            received.append((moved, index - distance))
        work = yield received
        block = after(block, work)


def shards(tokens, gain, w_query, w_key, w_value, w_out, segment_ids, page_table):
    half_rows = tokens.shape[0]
    block_rows = 2 * half_rows
    count = lax.axis_size("seq")
    index = lax.axis_index("seq")
    core = lax.axis_index("kv")
    reach = min(8, count // 2 - 1)

    normed = norm(tokens, gain)
    other_normed = swap_cores(normed)
    own_block = project_kv(normed, other_normed, w_key, w_value)

    if count == 2 * (reach + 1) and count // 2 == 8:
        exchanges = cube_exchanges(own_block, index, count)
    else:
        exchanges = distance_exchanges(own_block, index, count, reach)
    group = [(own_block, index)] + next(exchanges)

    query = project_query(normed, other_normed, w_query)

    offsets = jnp.arange(half_rows, dtype=jnp.int32)
    local = jnp.concatenate([core * half_rows + offsets, (1 - core) * half_rows + offsets])

    def positions(source):
        return (index if source is None else source) * block_rows + local

    def segs(source):
        start = jnp.maximum(index if source is None else source, 0) * block_rows
        first = lax.dynamic_slice_in_dim(segment_ids, start + core * half_rows, half_rows)
        second = lax.dynamic_slice_in_dim(segment_ids, start + (1 - core) * half_rows, half_rows)
        found = jnp.concatenate([first, second])
        return found if source is None else jnp.where(source >= 0, found, -1)

    heads = own_block.shape[0]
    pages = own_block.reshape(heads, 2, 2, half_rows, HD).transpose(2, 1, 0, 3, 4)
    own_slot = lax.dynamic_index_in_dim(page_table, core, keepdims=False)
    page_pool = jnp.where(own_slot == 0, pages, pages[::-1])

    state, done = None, query
    while group:
        blocks = [block for block, _ in group]
        sources = [source for _, source in group]
        try:
            following = exchanges.send(done)
        except StopIteration:
            following = None
        state = attend(query, blocks, sources, segs, positions, state, following is None)
        group, done = following, (state, page_pool)
    attention = state

    pieces = 2
    parts = [project_out(attention, w_out, piece, pieces) for piece in range(pieces)]
    mine = [part for part, _ in parts]
    theirs = [swap_cores(part) for _, part in parts]
    mixed, attn_out = finish(tokens, mine, theirs)
    return (mixed, attn_out, page_pool)


def solution(mesh):
    in_specs = (
        P(("seq", "kv"), None),
        P(),
        P(None, "kv"),
        P(None, "kv"),
        P(None, "kv"),
        P("kv", None),
        P(),
        P("seq"),
    )
    out_specs = (P(("seq", "kv"), None), P(("seq", "kv"), None), P("seq", None, "kv", None, None))
    return jax.shard_map(shards, mesh=mesh, in_specs=in_specs, out_specs=out_specs, check_vma=False)
```

```python
import functools
import math
import typing

import jax
import jax.numpy as jnp
from jax import lax
from jax.experimental import pallas as pl
from jax.experimental.pallas import tpu as pltpu
from jax.sharding import PartitionSpec as P

HD = 128
NORM_EPS = 1e-05
MASKED = -1e30
MIB = 1024 * 1024


IN_VMEM = pl.BlockSpec(memory_space=pltpu.VMEM)
IN_PLACE = pl.BlockSpec(memory_space=pltpu.HBM)


def call(
    kernel,
    name,
    args,
    outs,
    flops,
    limit=8,
    scratch=(),
    in_specs=None,
    out_specs=IN_VMEM,
    exps=0,
    aliases=None,
):
    outs_list = outs if isinstance(outs, list) else [outs]
    moved = sum(math.prod(a.shape) * a.dtype.itemsize for a in list(args) + outs_list)
    return pl.pallas_call(
        kernel,
        in_specs=in_specs or [IN_VMEM] * len(args),
        out_specs=jax.tree.map(lambda _: out_specs, outs),
        out_shape=outs,
        scratch_shapes=scratch,
        input_output_aliases=aliases or {},
        compiler_params=pltpu.CompilerParams(vmem_limit_bytes=limit * MIB),
        cost_estimate=pl.CostEstimate(flops=flops, bytes_accessed=moved, transcendentals=exps),
        name=name,
    )(
        *(
            pltpu.with_memory_space_constraint(arg, pltpu.HBM) if spec is IN_PLACE else arg
            for arg, spec in zip(args, in_specs or [IN_VMEM] * len(args))
        )
    )


def norm_rows(x_ref, gain_ref, out_ref, first):
    step = 16
    for start in range(0, x_ref.shape[0], step):
        wide = x_ref[start : start + step, :].astype(jnp.float32)
        mean = jnp.mean(wide * wide, axis=1, keepdims=True)
        normed = wide * lax.rsqrt(mean + NORM_EPS) * gain_ref[...]
        out_ref[first + start : first + start + step, :] = normed.astype(jnp.bfloat16)


def stream(copies, ahead, use):
    for n in range(min(ahead, len(copies))):
        for copy in copies[n]:
            copy.start()
    for n in range(len(copies)):
        for copy in copies[n]:
            copy.wait()
        if n + ahead < len(copies):
            for copy in copies[n + ahead]:
                copy.start()
        use(n)


def project_kv_kernel(
    tokens_hbm, gain_hbm, wk_hbm, wv_hbm, other_ref, normed_ref, kv_ref,
    x_ref, gain_ref, wk_ref, wv_ref, sems,
):
    half = x_ref.shape[0]
    pairs = ((tokens_hbm, x_ref), (gain_hbm, gain_ref), (wk_hbm, wk_ref), (wv_hbm, wv_ref))
    copies = [pltpu.make_async_copy(*pair, sems.at[n]) for n, pair in enumerate(pairs)]
    for copy in copies:
        copy.start()
    copies[1].wait()
    norm_rows(other_ref, gain_ref, normed_ref, half)
    copies[0].wait()
    norm_rows(x_ref, gain_ref, normed_ref, 0)
    for n, ref in enumerate((wk_ref, wv_ref)):
        copies[2 + n].wait()
        part = jnp.dot(normed_ref[...], ref[...], preferred_element_type=jnp.float32)
        for head in range(kv_ref.shape[0]):
            kv_ref[head, n] = part[:, head * HD : (head + 1) * HD].astype(kv_ref.dtype)


def project_kv(tokens, other_tokens, gain, w_key, w_value):
    half, width = tokens.shape
    heads = w_key.shape[1] // HD
    outs = [
        jax.ShapeDtypeStruct((2 * half, width), jnp.bfloat16),
        jax.ShapeDtypeStruct((heads, 2, 2 * half, HD), jnp.bfloat16),
    ]
    return call(
        project_kv_kernel,
        "project_kv",
        (tokens, gain[None, :], w_key, w_value, other_tokens),
        outs,
        8 * half * width * heads * HD,
        limit=14,
        scratch=[
            pltpu.VMEM(tokens.shape, tokens.dtype),
            pltpu.VMEM((1, width), jnp.float32),
            pltpu.VMEM(w_key.shape, w_key.dtype),
            pltpu.VMEM(w_value.shape, w_value.dtype),
            pltpu.SemaphoreType.DMA((4,)),
        ],
        in_specs=[IN_PLACE] * 4 + [IN_VMEM],
    )


def project_query_kernel(depth, x_ref, w_hbm, out_ref, w_ref, acc_ref, sems):
    chunks = w_ref.shape[0] // depth
    copies = []
    for n in range(chunks):
        rows = slice(n * depth, (n + 1) * depth)
        copies.append([pltpu.make_async_copy(w_hbm.at[rows], w_ref.at[rows], sems.at[n])])

    def use(n):
        rows = slice(n * depth, (n + 1) * depth)
        tile = 512
        for start in range(0, out_ref.shape[1], tile):
            cols = slice(start, start + tile)
            part = jnp.dot(
                x_ref[:, rows], w_ref[rows, cols], preferred_element_type=jnp.float32
            )
            if n:
                part = part + acc_ref[:, cols]
            if n < chunks - 1:
                acc_ref[:, cols] = part
            else:
                out_ref[:, cols] = part.astype(out_ref.dtype)

    stream(copies, 3, use)


def project_query(normed, w_query, depth=512):
    out = (normed.shape[0], w_query.shape[1])
    return call(
        functools.partial(project_query_kernel, depth),
        "project_query",
        (normed, w_query),
        jax.ShapeDtypeStruct(out, jnp.bfloat16),
        2 * normed.shape[0] * w_query.size,
        limit=22,
        scratch=[
            pltpu.VMEM(w_query.shape, w_query.dtype),
            pltpu.VMEM(out, jnp.float32),
            pltpu.SemaphoreType.DMA((w_query.shape[0] // depth,)),
        ],
        in_specs=[IN_VMEM, IN_PLACE],
    )


def attention_kernel(block_count, first, last, group, *refs):
    seg_q, pos_q, seg_k, pos_k, q_ref = refs[:5]
    blocks = refs[5 : 5 + block_count]
    refs = refs[5 + block_count :]
    if not first:
        acc_in, peak_in, mass_in = refs[:3]
        refs = refs[3:]
    if last:
        out_ref, bias_ref = refs
    else:
        acc_out, peak_out, mass_out, bias_ref = refs
    seen = (seg_q[...] == seg_k[...]) & (pos_k[...] <= pos_q[...])
    bias_ref[...] = jnp.where(seen, 0.0, MASKED)
    rows = q_ref.shape[0]
    width = seg_k.shape[1]
    factor = math.log2(math.e) / math.sqrt(HD)
    for head in range(q_ref.shape[1] // HD):
        if head % group == 0:
            keys = jnp.concatenate([block[head // group, 0] for block in blocks], axis=0)
            values = jnp.concatenate([block[head // group, 1] for block in blocks], axis=0)
            values = jnp.concatenate([values, jnp.ones_like(values)], axis=1)
        cols = slice(head * HD, (head + 1) * HD)
        scores = lax.dot_general(
            q_ref[:, cols], keys, (((1,), (1,)), ((), ())), preferred_element_type=jnp.float32
        )
        scores = scores + bias_ref[...]
        peak = jnp.broadcast_to(jnp.max(scores, axis=1, keepdims=True), (rows, HD))
        if not first:
            old = peak_in[:, cols]
            peak = jnp.maximum(peak, old)
        shift = peak * factor
        weights = jnp.concatenate(
            [
                jnp.exp2(scores[:, at : at + HD] * factor - shift).astype(jnp.bfloat16)
                for at in range(0, width, HD)
            ],
            axis=1,
        )
        total = jnp.dot(weights, values, preferred_element_type=jnp.float32)
        acc = total[:, :HD]
        mass = total[:, HD:]
        if not first:
            keep = jnp.exp2((old - peak) * factor)
            acc = acc + acc_in[:, cols] * keep
            mass = mass + mass_in[:, cols] * keep
        if last:
            out_ref[:, cols] = (acc / mass).astype(jnp.bfloat16)
        else:
            acc_out[:, cols] = acc
            peak_out[:, cols] = peak
            mass_out[:, cols] = mass


def attend(query, query_labels, blocks, key_labels, group, state, last):
    rows, q_cols = query.shape
    seg_k, pos_k = (jnp.concatenate(parts)[None, :] for parts in zip(*key_labels))
    seg_q, pos_q = (part[:, None] for part in query_labels)
    keys = len(blocks) * rows
    args = [seg_q, pos_q, seg_k, pos_k, query]
    args += [block.block if isinstance(block, Farthest) else block for block in blocks]
    first = state is None
    args += [] if first else state
    if last:
        outs = jax.ShapeDtypeStruct((rows, q_cols), jnp.bfloat16)
    else:
        outs = [jax.ShapeDtypeStruct((rows, q_cols), jnp.float32)] * 3
    return call(
        functools.partial(attention_kernel, len(blocks), first, last, group),
        "attend",
        args,
        outs,
        6 * rows * keys * q_cols,
        limit=14,
        scratch=[pltpu.VMEM((rows, keys), jnp.float32)],
        exps=rows * keys * q_cols // HD,
    )


def project_out_kernel(pieces, x_ref, w_ref, own_ref, other_ref, *, piece):
    half = own_ref.shape[0]
    cols = own_ref.shape[1]
    tile = 512
    for start in range(0, cols, tile):
        at = piece * cols + start
        part = jnp.dot(
            x_ref[...], w_ref[:, at : at + tile], preferred_element_type=jnp.float32
        )
        own_ref[:, start : start + tile] = part[:half]
        other_ref[:, start : start + tile] = part[half:].astype(other_ref.dtype)


def project_out(attention, w_out, piece, pieces):
    rows, depth = attention.shape
    cols = w_out.shape[1] // pieces
    outs = [
        jax.ShapeDtypeStruct((rows // 2, cols), jnp.float32),
        jax.ShapeDtypeStruct((rows // 2, cols), jnp.bfloat16),
    ]
    return call(
        functools.partial(project_out_kernel, pieces, piece=piece),
        "project_out",
        (attention, w_out),
        outs,
        2 * rows * depth * cols,
    )


def finish_kernel(piece, tokens_ref, mine, theirs, *refs):
    mixed_hbm, out_hbm, mixed, out, sems = refs[-5:]
    at = slice(piece * mine.shape[1], (piece + 1) * mine.shape[1])
    branch = mine[...] + theirs[...].astype(jnp.float32)
    out[...] = branch.astype(out.dtype)
    out_copy = pltpu.make_async_copy(out, out_hbm.at[:, at], sems.at[0])
    out_copy.start()
    mixed[...] = (tokens_ref[:, at].astype(jnp.float32) + branch).astype(mixed.dtype)
    mixed_copy = pltpu.make_async_copy(mixed, mixed_hbm.at[:, at], sems.at[1])
    mixed_copy.start()
    out_copy.wait()
    mixed_copy.wait()


def finish(tokens, mine, theirs, piece, before):
    outs = [jax.ShapeDtypeStruct(tokens.shape, jnp.bfloat16)] * 2
    return call(
        functools.partial(finish_kernel, piece),
        "finish",
        (tokens, mine, theirs, *before),
        outs,
        2 * tokens.size,
        scratch=[
            pltpu.VMEM(mine.shape, jnp.bfloat16),
            pltpu.VMEM(mine.shape, jnp.bfloat16),
            pltpu.SemaphoreType.DMA((2,)),
        ],
        in_specs=[IN_VMEM] * 3 + [IN_PLACE] * len(before),
        out_specs=IN_PLACE,
        aliases={3 + n: n for n in range(len(before))},
    )


def after(values, *others):
    return lax.optimization_barrier((values, others))[0]


def swap_cores(value):
    return lax.ppermute(value, "kv", [(0, 1), (1, 0)])


class Farthest(typing.NamedTuple):
    block: jax.Array
    first: jax.Array


def cube_exchanges(block, index, core, count):
    half = count // 2
    rows = block.shape[2]
    page = rows // 2

    def exchange(value, bit):
        return lax.ppermute(value, "seq", [(i, i ^ bit) for i in range(count)])

    from_x, from_y, from_z = exchange(block, 1), exchange(block, 2), exchange(block, 4)
    work = yield [(from_x, index ^ 1), (from_y, index ^ 2), (from_z, index ^ 4)]
    from_x, from_y, from_z = after((from_x, from_y, from_z), work)
    from_xy, from_yz, from_xz = exchange(from_y, 1), exchange(from_z, 2), exchange(from_x, 4)
    work = yield [(from_xy, index ^ 3), (from_yz, index ^ 6), (from_xz, index ^ 5)]
    from_xy, from_yz, from_xz = after((from_xy, from_yz, from_xz), work)
    seam_page = lax.dynamic_slice_in_dim(from_xy, (1 - core) * page, page, 2)
    up = jnp.where(
        index % half == half // 2,
        seam_page.reshape(-1, HD),
        from_xy[2:].reshape(-1, HD),
    )
    swapped = {}
    for low in range(half // 2, count, half):
        swapped[low] = (low + half // 2) % count
    pairs = [(i, swapped.get(i, i ^ 4)) for i in range(count)]
    part_x, part_y = exchange(from_yz[:1], 1), exchange(from_xz[1:2], 2)
    part_z = lax.ppermute(up, "seq", pairs)
    first = index % half == 0
    usual = jnp.concatenate([part_x, part_y, part_z.reshape(2, 2, rows, HD)])
    before = part_z.reshape(4, 2, page, HD)
    before = jnp.concatenate([before, before], axis=2)
    yield [(Farthest(jnp.where(first, before, usual), first), index ^ 7)]


def distance_exchanges(block, index, count, reach):
    step = 3
    for start in range(1, reach + 1, step):
        received = []
        for distance in range(start, min(start + step, reach + 1)):
            moved = lax.ppermute(block, "seq", [(i, i + distance) for i in range(count - distance)])
            received.append((moved, index - distance))
        work = yield received
        block = after(block, work)


def shards(tokens, gain, w_query, w_key, w_value, w_out, segment_ids, page_table):
    half_rows = tokens.shape[0]
    block_rows = 2 * half_rows
    count = lax.axis_size("seq")
    index = lax.axis_index("seq")
    core = lax.axis_index("kv")
    reach = min(8, count // 2 - 1)

    other_tokens = swap_cores(tokens)
    normed, own_block = project_kv(tokens, other_tokens, gain, w_key, w_value)

    if count == 2 * (reach + 1) and count // 2 == 8:
        exchanges = cube_exchanges(own_block, index, core, count)
    else:
        exchanges = distance_exchanges(own_block, index, count, reach)
    group = [(own_block, index)] + next(exchanges)

    query = project_query(normed, w_query)

    offsets = jnp.arange(half_rows, dtype=jnp.int32)
    local = jnp.concatenate([core * half_rows + offsets, (1 - core) * half_rows + offsets])

    def labels(source):
        starts = (core * half_rows, (1 - core) * half_rows)
        begin = jnp.maximum(source, 0) * block_rows
        found = [lax.dynamic_slice_in_dim(segment_ids, begin + s, half_rows) for s in starts]
        return jnp.where(source >= 0, jnp.concatenate(found), -1), source * block_rows + local

    def labels_before():
        begin = index * block_rows - half_rows
        found = lax.dynamic_slice_in_dim(segment_ids, jnp.maximum(begin, 0), half_rows)
        nothing = jnp.full((half_rows,), -1, jnp.int32)
        segs = jnp.concatenate([jnp.where(index > 0, found, -1), nothing])
        return segs, jnp.concatenate([begin + offsets, begin + offsets])

    def key_labels(block, source):
        if not isinstance(block, Farthest):
            return labels(source)
        return jax.tree.map(
            lambda before, usual: jnp.where(block.first, before, usual),
            labels_before(),
            labels(source),
        )

    heads = own_block.shape[0]
    pages = own_block.reshape(heads, 2, 2, half_rows, HD).transpose(2, 1, 0, 3, 4)
    own_slot = lax.dynamic_index_in_dim(page_table, core, keepdims=False)
    page_pool = jnp.where(own_slot == 0, pages, pages[::-1])

    groups = query.shape[1] // HD // heads
    state, done = None, query
    while group:
        blocks = [block for block, _ in group]
        keys = [key_labels(block, source) for block, source in group]
        try:
            following = exchanges.send(done)
        except StopIteration:
            following = None
        state = attend(
            query, labels(index), blocks, keys, groups, state, following is None
        )
        group, done = following, (state, page_pool)
    attention = state

    pieces = 2
    parts = [project_out(attention, w_out, piece, pieces) for piece in range(pieces)]
    results = ()
    for piece, (mine, theirs) in enumerate(parts):
        results = finish(tokens, mine, swap_cores(theirs), piece, results)
    mixed, attn_out = results
    return (mixed, attn_out, page_pool)


def solution(mesh):
    in_specs = (
        P(("seq", "kv"), None),
        P(),
        P(None, "kv"),
        P(None, "kv"),
        P(None, "kv"),
        P("kv", None),
        P(),
        P("seq"),
    )
    out_specs = (P(("seq", "kv"), None), P(("seq", "kv"), None), P("seq", None, "kv", None, None))
    return jax.shard_map(shards, mesh=mesh, in_specs=in_specs, out_specs=out_specs, check_vma=False)
```

```python
import functools
import math
import typing

import jax
import jax.numpy as jnp
from jax import lax
from jax.experimental import pallas as pl
from jax.experimental.pallas import tpu as pltpu
from jax.sharding import PartitionSpec as P

HD = 128
NORM_EPS = 1e-05
MASKED = -1e30
MIB = 1024 * 1024


IN_VMEM = pl.BlockSpec(memory_space=pltpu.VMEM)
IN_PLACE = pl.BlockSpec(memory_space=pltpu.HBM)


def call(
    kernel,
    name,
    args,
    outs,
    flops,
    limit=8,
    scratch=(),
    in_specs=None,
    out_specs=IN_VMEM,
    exps=0,
    aliases=None,
):
    outs_list = outs if isinstance(outs, list) else [outs]
    moved = sum(math.prod(a.shape) * a.dtype.itemsize for a in list(args) + outs_list)
    return pl.pallas_call(
        kernel,
        in_specs=in_specs or [IN_VMEM] * len(args),
        out_specs=jax.tree.map(lambda _: out_specs, outs),
        out_shape=outs,
        scratch_shapes=scratch,
        input_output_aliases=aliases or {},
        compiler_params=pltpu.CompilerParams(vmem_limit_bytes=limit * MIB),
        cost_estimate=pl.CostEstimate(flops=flops, bytes_accessed=moved, transcendentals=exps),
        name=name,
    )(
        *(
            pltpu.with_memory_space_constraint(arg, pltpu.HBM) if spec is IN_PLACE else arg
            for arg, spec in zip(args, in_specs or [IN_VMEM] * len(args))
        )
    )


def norm_rows(x_ref, gain_ref, out_ref):
    step = 16
    for start in range(0, x_ref.shape[0], step):
        wide = x_ref[start : start + step, :].astype(jnp.float32)
        mean = jnp.mean(wide * wide, axis=1, keepdims=True)
        normed = wide * lax.rsqrt(mean + NORM_EPS) * gain_ref[...]
        out_ref[start : start + step, :] = normed.astype(jnp.bfloat16)


def stream(copies, ahead, use):
    for n in range(min(ahead, len(copies))):
        for copy in copies[n]:
            copy.start()
    for n in range(len(copies)):
        for copy in copies[n]:
            copy.wait()
        if n + ahead < len(copies):
            for copy in copies[n + ahead]:
                copy.start()
        use(n)


def stage_kernel(
    tokens_hbm, gain_hbm, wk_hbm, wv_hbm, normed_ref, gain_ref, wk_ref, wv_ref, x_ref, sems
):
    pairs = ((tokens_hbm, x_ref), (gain_hbm, gain_ref), (wk_hbm, wk_ref), (wv_hbm, wv_ref))
    copies = [pltpu.make_async_copy(*pair, sems.at[n]) for n, pair in enumerate(pairs)]
    for copy in copies:
        copy.start()
    copies[0].wait()
    copies[1].wait()
    norm_rows(x_ref, gain_ref, normed_ref)
    copies[2].wait()
    copies[3].wait()


def stage(tokens, gain, w_key, w_value):
    gain = gain[None, :]
    return call(
        stage_kernel,
        "stage",
        (tokens, gain, w_key, w_value),
        [jax.ShapeDtypeStruct(a.shape, a.dtype) for a in (tokens, gain, w_key, w_value)],
        4 * tokens.size,
        scratch=[pltpu.VMEM(tokens.shape, tokens.dtype), pltpu.SemaphoreType.DMA((4,))],
        in_specs=[IN_PLACE] * 4,
    )


def project_kv_kernel(own_ref, other_ref, gain_ref, wk_ref, wv_ref, normed_ref, kv_ref):
    norm_rows(other_ref, gain_ref, normed_ref)
    rows = jnp.concatenate([own_ref[...], normed_ref[...]], axis=0)
    for head in range(kv_ref.shape[0]):
        cols = slice(head * HD, (head + 1) * HD)
        weights = jnp.concatenate([wk_ref[:, cols], wv_ref[:, cols]], axis=1)
        pair = jnp.dot(rows, weights, preferred_element_type=jnp.float32).astype(jnp.bfloat16)
        kv_ref[head, 0] = pair[:, :HD]
        kv_ref[head, 1] = pair[:, HD:]


def project_kv(normed, other_tokens, gain, w_key, w_value):
    half, width = normed.shape
    heads = w_key.shape[1] // HD
    outs = [
        jax.ShapeDtypeStruct((half, width), jnp.bfloat16),
        jax.ShapeDtypeStruct((heads, 2, 2 * half, HD), jnp.bfloat16),
    ]
    flops = 8 * half * width * heads * HD
    args = (normed, other_tokens, gain, w_key, w_value)
    return call(project_kv_kernel, "project_kv", args, outs, flops)


def project_query_kernel(depth, own_ref, other_ref, w_hbm, out_ref, w_ref, acc_ref, sems):
    chunks = w_ref.shape[0] // depth
    copies = []
    for n in range(chunks):
        rows = slice(n * depth, (n + 1) * depth)
        copies.append([pltpu.make_async_copy(w_hbm.at[rows], w_ref.at[rows], sems.at[n])])

    def use(n):
        rows = slice(n * depth, (n + 1) * depth)
        x = jnp.concatenate([own_ref[:, rows], other_ref[:, rows]], axis=0)
        tile = 512
        for start in range(0, out_ref.shape[1], tile):
            cols = slice(start, start + tile)
            part = jnp.dot(x, w_ref[rows, cols], preferred_element_type=jnp.float32)
            if n:
                part = part + acc_ref[:, cols]
            if n < chunks - 1:
                acc_ref[:, cols] = part
            else:
                out_ref[:, cols] = part.astype(out_ref.dtype)

    stream(copies, 3, use)


def project_query(own, other, w_query, depth=512):
    out = (2 * own.shape[0], w_query.shape[1])
    return call(
        functools.partial(project_query_kernel, depth),
        "project_query",
        (own, other, w_query),
        jax.ShapeDtypeStruct(out, jnp.bfloat16),
        4 * own.shape[0] * w_query.size,
        limit=22,
        scratch=[
            pltpu.VMEM(w_query.shape, w_query.dtype),
            pltpu.VMEM(out, jnp.float32),
            pltpu.SemaphoreType.DMA((w_query.shape[0] // depth,)),
        ],
        in_specs=[IN_VMEM, IN_VMEM, IN_PLACE],
    )


def attention_kernel(block_count, first, last, group, *refs):
    seg_q, pos_q, seg_k, pos_k, q_ref = refs[:5]
    blocks = refs[5 : 5 + block_count]
    refs = refs[5 + block_count :]
    if not first:
        acc_in, peak_in, mass_in = refs[:3]
        refs = refs[3:]
    if last:
        out_ref, bias_ref = refs
    else:
        acc_out, peak_out, mass_out, bias_ref = refs
    seen = (seg_q[...] == seg_k[...]) & (pos_k[...] <= pos_q[...])
    bias_ref[...] = jnp.where(seen, 0.0, MASKED)
    rows = q_ref.shape[0]
    width = seg_k.shape[1]
    factor = math.log2(math.e) / math.sqrt(HD)
    heads = q_ref.shape[1] // HD
    cols = [slice(head * HD, (head + 1) * HD) for head in range(heads)]
    pairs = {}

    def key_values(head):
        which = head // group
        if which not in pairs:
            keys = jnp.concatenate([block[which, 0] for block in blocks], axis=0)
            values = jnp.concatenate([block[which, 1] for block in blocks], axis=0)
            pairs[which] = keys, jnp.concatenate([values, jnp.ones_like(values)], axis=1)
        return pairs[which]

    def score(head):
        keys = key_values(head)[0]
        scores = lax.dot_general(
            q_ref[:, cols[head]], keys, (((1,), (1,)), ((), ())), preferred_element_type=jnp.float32
        )
        return scores + bias_ref[...]

    def weigh(head, scores):
        peak = jnp.broadcast_to(jnp.max(scores, axis=1, keepdims=True), (rows, HD))
        if not first:
            peak = jnp.maximum(peak, peak_in[:, cols[head]])
        shift = peak * factor
        weights = [
            jnp.exp2(scores[:, at : at + HD] * factor - shift).astype(jnp.bfloat16)
            for at in range(0, width, HD)
        ]
        return peak, jnp.concatenate(weights, axis=1)

    def add_up(head, peak, weights):
        total = jnp.dot(weights, key_values(head)[1], preferred_element_type=jnp.float32)
        acc = total[:, :HD]
        mass = total[:, HD:]
        if not first:
            keep = jnp.exp2((peak_in[:, cols[head]] - peak) * factor)
            acc = acc + acc_in[:, cols[head]] * keep
            mass = mass + mass_in[:, cols[head]] * keep
        if last:
            out_ref[:, cols[head]] = (acc / mass).astype(jnp.bfloat16)
        else:
            acc_out[:, cols[head]] = acc
            peak_out[:, cols[head]] = peak
            mass_out[:, cols[head]] = mass

    if last:
        for start in range(0, heads, 4):
            many = range(start, start + 4)
            scores = [score(head) for head in many]
            weighed = [weigh(head, scores[head - start]) for head in many]
            for head in many:
                add_up(head, *weighed[head - start])
    else:
        ahead = score(0)
        for head in range(heads):
            scores, ahead = ahead, score(head + 1) if head + 1 < heads else None
            add_up(head, *weigh(head, scores))


def attend(query, query_labels, blocks, key_labels, group, state, last):
    rows, q_cols = query.shape
    seg_k, pos_k = (jnp.concatenate(parts)[None, :] for parts in zip(*key_labels))
    seg_q, pos_q = (part[:, None] for part in query_labels)
    keys = len(blocks) * rows
    args = [seg_q, pos_q, seg_k, pos_k, query]
    args += [block.block if isinstance(block, Farthest) else block for block in blocks]
    first = state is None
    args += [] if first else state
    if last:
        outs = jax.ShapeDtypeStruct((rows, q_cols), jnp.bfloat16)
    else:
        outs = [jax.ShapeDtypeStruct((rows, q_cols), jnp.float32)] * 3
    return call(
        functools.partial(attention_kernel, len(blocks), first, last, group),
        "attend",
        args,
        outs,
        6 * rows * keys * q_cols,
        limit=14,
        scratch=[pltpu.VMEM((rows, keys), jnp.float32)],
        exps=rows * keys * q_cols // HD,
    )


def project_out_kernel(first, x_ref, w_ref, own_ref, other_ref):
    half, cols = own_ref.shape
    tile = 512
    for start in range(0, cols, tile):
        weights = w_ref[:, first + start : first + start + tile]
        part = jnp.dot(x_ref[...], weights, preferred_element_type=jnp.float32)
        own_ref[:, start : start + tile] = part[:half]
        other_ref[:, start : start + tile] = part[half:].astype(other_ref.dtype)


def project_out(attention, w_out, first, cols):
    rows, depth = attention.shape
    outs = [
        jax.ShapeDtypeStruct((rows // 2, cols), jnp.float32),
        jax.ShapeDtypeStruct((rows // 2, cols), jnp.bfloat16),
    ]
    kernel = functools.partial(project_out_kernel, first)
    return call(kernel, "project_out", (attention, w_out), outs, 2 * rows * depth * cols)


def finish_kernel(parts, tokens_ref, *refs):
    mixed_hbm, out_hbm, mixed, out, sems = refs[2 * parts :]
    copies = []
    first = 0
    for part in range(parts):
        mine, theirs = refs[2 * part : 2 * part + 2]
        tile = 1024
        for start in range(0, mine.shape[1], tile):
            cols = slice(start, start + tile)
            at = slice(first + start, first + start + tile)
            branch = mine[:, cols] + theirs[:, cols].astype(jnp.float32)
            out[:, at] = branch.astype(out.dtype)
            mixed[:, at] = (tokens_ref[:, at].astype(jnp.float32) + branch).astype(mixed.dtype)
            for here, there in ((out, out_hbm), (mixed, mixed_hbm)):
                sem = sems.at[len(copies)]
                copies.append(pltpu.make_async_copy(here.at[:, at], there.at[:, at], sem))
                copies[-1].start()
        first += mine.shape[1]
    for copy in copies:
        copy.wait()


def finish(tokens, parts):
    args = [tokens] + [array for part in parts for array in part]
    return call(
        functools.partial(finish_kernel, len(parts)),
        "finish",
        args,
        [jax.ShapeDtypeStruct(tokens.shape, jnp.bfloat16)] * 2,
        2 * tokens.size,
        scratch=[
            pltpu.VMEM(tokens.shape, jnp.bfloat16),
            pltpu.VMEM(tokens.shape, jnp.bfloat16),
            pltpu.SemaphoreType.DMA((tokens.shape[1] // 512,)),
        ],
        out_specs=IN_PLACE,
    )


def after(values, *others):
    return lax.optimization_barrier((values, others))[0]


def swap_cores(value):
    return lax.ppermute(value, "kv", [(0, 1), (1, 0)])


class Farthest(typing.NamedTuple):
    block: jax.Array
    first: jax.Array


def cube_exchanges(block, index, core, count):
    half = count // 2
    rows = block.shape[2]
    page = rows // 2

    def exchange(value, bit):
        return lax.ppermute(value, "seq", [(i, i ^ bit) for i in range(count)])

    from_x, from_y, from_z = exchange(block, 1), exchange(block, 2), exchange(block, 4)
    work = yield [(from_x, index ^ 1), (from_y, index ^ 2), (from_z, index ^ 4)]
    from_x, from_y, from_z = (after(value, work) for value in (from_x, from_y, from_z))
    from_xz, from_xy, from_yz = exchange(from_x, 4), exchange(from_y, 1), exchange(from_z, 2)
    work = yield [(from_xy, index ^ 3), (from_yz, index ^ 6), (from_xz, index ^ 5)]
    from_xy, from_yz, from_xz = (after(value, work) for value in (from_xy, from_yz, from_xz))
    seam_page = lax.dynamic_slice_in_dim(from_xy, (1 - core) * page, page, 2)
    up = jnp.where(
        index % half == half // 2,
        seam_page.reshape(-1, HD),
        from_xy[2:].reshape(-1, HD),
    )
    swapped = {}
    for low in range(half // 2, count, half):
        swapped[low] = (low + half // 2) % count
    pairs = [(i, swapped.get(i, i ^ 4)) for i in range(count)]
    part_x, part_y = exchange(from_yz[:1], 1), exchange(from_xz[1:2], 2)
    part_z = lax.ppermute(up, "seq", pairs)
    first = index % half == 0
    usual = jnp.concatenate([part_x, part_y, part_z.reshape(2, 2, rows, HD)])
    before = part_z.reshape(4, 2, page, HD)
    before = jnp.concatenate([before, before], axis=2)
    yield [(Farthest(jnp.where(first, before, usual), first), index ^ 7)]


def distance_exchanges(block, index, count, reach):
    step = 3
    for start in range(1, reach + 1, step):
        received = []
        for distance in range(start, min(start + step, reach + 1)):
            moved = lax.ppermute(block, "seq", [(i, i + distance) for i in range(count - distance)])
            received.append((moved, index - distance))
        work = yield received
        block = after(block, work)


def shards(tokens, gain, w_query, w_key, w_value, w_out, segment_ids, page_table):
    half_rows = tokens.shape[0]
    block_rows = 2 * half_rows
    count = lax.axis_size("seq")
    index = lax.axis_index("seq")
    core = lax.axis_index("kv")
    reach = min(8, count // 2 - 1)

    other_tokens = swap_cores(tokens)
    normed, staged_gain, staged_key, staged_value = stage(tokens, gain, w_key, w_value)
    other_normed, own_block = project_kv(
        normed, other_tokens, staged_gain, staged_key, staged_value
    )
    page_table, index, core = after((page_table, index, core), own_block)

    if count == 2 * (reach + 1) and count // 2 == 8:
        exchanges = cube_exchanges(own_block, index, core, count)
    else:
        exchanges = distance_exchanges(own_block, index, count, reach)
    group = [(own_block, index)] + next(exchanges)

    query = project_query(normed, other_normed, w_query)

    offsets = jnp.arange(half_rows, dtype=jnp.int32)
    local = jnp.concatenate([core * half_rows + offsets, (1 - core) * half_rows + offsets])

    def labels(source):
        starts = (core * half_rows, (1 - core) * half_rows)
        begin = jnp.maximum(source, 0) * block_rows
        found = [lax.dynamic_slice_in_dim(segment_ids, begin + s, half_rows) for s in starts]
        return jnp.where(source >= 0, jnp.concatenate(found), -1), source * block_rows + local

    def labels_before():
        begin = index * block_rows - half_rows
        found = lax.dynamic_slice_in_dim(segment_ids, jnp.maximum(begin, 0), half_rows)
        nothing = jnp.full((half_rows,), -1, jnp.int32)
        segs = jnp.concatenate([jnp.where(index > 0, found, -1), nothing])
        return segs, jnp.concatenate([begin + offsets, begin + offsets])

    def key_labels(block, source):
        if not isinstance(block, Farthest):
            return labels(source)
        return jax.tree.map(
            lambda before, usual: jnp.where(block.first, before, usual),
            labels_before(),
            labels(source),
        )

    heads = own_block.shape[0]
    pages = own_block.reshape(heads, 2, 2, half_rows, HD).transpose(2, 1, 0, 3, 4)
    own_slot = lax.dynamic_index_in_dim(page_table, core, keepdims=False)
    page_pool = jnp.where(own_slot == 0, pages, pages[::-1])

    groups = query.shape[1] // HD // heads
    state, done = None, query
    while group:
        blocks = [block for block, _ in group]
        keys = [key_labels(block, source) for block, source in group]
        try:
            following = exchanges.send(done)
        except StopIteration:
            following = None
        state = attend(
            query, labels(index), blocks, keys, groups, state, following is None
        )
        group, done = following, (state, page_pool)
    attention = state

    width = w_out.shape[1]
    cuts = [0, width * 3 // 4, width]
    parts = []
    for first, end in zip(cuts, cuts[1:]):
        mine, theirs = project_out(attention, w_out, first, end - first)
        parts.append((mine, swap_cores(theirs)))
    mixed, attn_out = finish(tokens, parts)
    return (mixed, attn_out, page_pool)


def solution(mesh):
    in_specs = (
        P(("seq", "kv"), None),
        P(),
        P(None, "kv"),
        P(None, "kv"),
        P(None, "kv"),
        P("kv", None),
        P(),
        P("seq"),
    )
    out_specs = (P(("seq", "kv"), None), P(("seq", "kv"), None), P("seq", None, "kv", None, None))
    return jax.shard_map(shards, mesh=mesh, in_specs=in_specs, out_specs=out_specs, check_vma=False)
```

```python
import functools
import math
import typing

import jax
import jax.numpy as jnp
from jax import lax
from jax.experimental import pallas as pl
from jax.experimental.pallas import tpu as pltpu
from jax.sharding import PartitionSpec as P

HD = 128
NORM_EPS = 1e-05
MASKED = -1e30
MIB = 1024 * 1024


IN_VMEM = pl.BlockSpec(memory_space=pltpu.VMEM)
IN_PLACE = pl.BlockSpec(memory_space=pltpu.HBM)


def call(
    kernel,
    name,
    args,
    outs,
    flops,
    limit=8,
    scratch=(),
    in_specs=None,
    out_specs=IN_VMEM,
    exps=0,
    aliases=None,
):
    outs_list = outs if isinstance(outs, list) else [outs]
    moved = sum(math.prod(a.shape) * a.dtype.itemsize for a in list(args) + outs_list)
    return pl.pallas_call(
        kernel,
        in_specs=in_specs or [IN_VMEM] * len(args),
        out_specs=jax.tree.map(lambda _: out_specs, outs),
        out_shape=outs,
        scratch_shapes=scratch,
        input_output_aliases=aliases or {},
        compiler_params=pltpu.CompilerParams(vmem_limit_bytes=limit * MIB),
        cost_estimate=pl.CostEstimate(flops=flops, bytes_accessed=moved, transcendentals=exps),
        name=name,
    )(
        *(
            pltpu.with_memory_space_constraint(arg, pltpu.HBM) if spec is IN_PLACE else arg
            for arg, spec in zip(args, in_specs or [IN_VMEM] * len(args))
        )
    )


def norm_rows(x_ref, gain_ref, out_ref):
    step = 16
    for start in range(0, x_ref.shape[0], step):
        wide = x_ref[start : start + step, :].astype(jnp.float32)
        mean = jnp.mean(wide * wide, axis=1, keepdims=True)
        normed = wide * lax.rsqrt(mean + NORM_EPS) * gain_ref[...]
        out_ref[start : start + step, :] = normed.astype(jnp.bfloat16)


def stream(copies, ahead, use):
    for n in range(min(ahead, len(copies))):
        for copy in copies[n]:
            copy.start()
    for n in range(len(copies)):
        for copy in copies[n]:
            copy.wait()
        if n + ahead < len(copies):
            for copy in copies[n + ahead]:
                copy.start()
        use(n)


def stage_kernel(
    tokens_hbm, gain_hbm, wk_hbm, wv_hbm, normed_ref, gain_ref, wk_ref, wv_ref, x_ref, sems
):
    pairs = ((tokens_hbm, x_ref), (gain_hbm, gain_ref), (wk_hbm, wk_ref), (wv_hbm, wv_ref))
    copies = [pltpu.make_async_copy(*pair, sems.at[n]) for n, pair in enumerate(pairs)]
    for copy in copies:
        copy.start()
    copies[0].wait()
    copies[1].wait()
    norm_rows(x_ref, gain_ref, normed_ref)
    copies[2].wait()
    copies[3].wait()


def stage(tokens, gain, w_key, w_value):
    gain = gain[None, :]
    return call(
        stage_kernel,
        "stage",
        (tokens, gain, w_key, w_value),
        [jax.ShapeDtypeStruct(a.shape, a.dtype) for a in (tokens, gain, w_key, w_value)],
        4 * tokens.size,
        scratch=[pltpu.VMEM(tokens.shape, tokens.dtype), pltpu.SemaphoreType.DMA((4,))],
        in_specs=[IN_PLACE] * 4,
    )


def project_kv_kernel(own_ref, other_ref, gain_ref, wk_ref, wv_ref, normed_ref, kv_ref):
    norm_rows(other_ref, gain_ref, normed_ref)
    rows = jnp.concatenate([own_ref[...], normed_ref[...]], axis=0)
    for head in range(kv_ref.shape[0]):
        cols = slice(head * HD, (head + 1) * HD)
        weights = jnp.concatenate([wk_ref[:, cols], wv_ref[:, cols]], axis=1)
        pair = jnp.dot(rows, weights, preferred_element_type=jnp.float32).astype(jnp.bfloat16)
        kv_ref[head, 0] = pair[:, :HD]
        kv_ref[head, 1] = pair[:, HD:]


def project_kv(normed, other_tokens, gain, w_key, w_value):
    half, width = normed.shape
    heads = w_key.shape[1] // HD
    outs = [
        jax.ShapeDtypeStruct((half, width), jnp.bfloat16),
        jax.ShapeDtypeStruct((heads, 2, 2 * half, HD), jnp.bfloat16),
    ]
    flops = 8 * half * width * heads * HD
    args = (normed, other_tokens, gain, w_key, w_value)
    return call(project_kv_kernel, "project_kv", args, outs, flops)


def project_query_kernel(depth, own_ref, other_ref, w_hbm, out_ref, w_ref, acc_ref, sems):
    chunks = w_ref.shape[0] // depth
    copies = []
    for n in range(chunks):
        rows = slice(n * depth, (n + 1) * depth)
        copies.append([pltpu.make_async_copy(w_hbm.at[rows], w_ref.at[rows], sems.at[n])])

    def use(n):
        rows = slice(n * depth, (n + 1) * depth)
        x = jnp.concatenate([own_ref[:, rows], other_ref[:, rows]], axis=0)
        tile = 512
        for start in range(0, out_ref.shape[1], tile):
            cols = slice(start, start + tile)
            part = jnp.dot(x, w_ref[rows, cols], preferred_element_type=jnp.float32)
            if n:
                part = part + acc_ref[:, cols]
            if n < chunks - 1:
                acc_ref[:, cols] = part
            else:
                out_ref[:, cols] = part.astype(out_ref.dtype)

    stream(copies, 3, use)


def project_query(own, other, w_query, depth=512):
    out = (2 * own.shape[0], w_query.shape[1])
    return call(
        functools.partial(project_query_kernel, depth),
        "project_query",
        (own, other, w_query),
        jax.ShapeDtypeStruct(out, jnp.bfloat16),
        4 * own.shape[0] * w_query.size,
        limit=22,
        scratch=[
            pltpu.VMEM(w_query.shape, w_query.dtype),
            pltpu.VMEM(out, jnp.float32),
            pltpu.SemaphoreType.DMA((w_query.shape[0] // depth,)),
        ],
        in_specs=[IN_VMEM, IN_VMEM, IN_PLACE],
    )


def attention_kernel(block_count, first, last, group, *refs):
    seg_q, pos_q, seg_k, pos_k, q_ref = refs[:5]
    blocks = refs[5 : 5 + block_count]
    refs = refs[5 + block_count :]
    if not first:
        acc_in, peak_in, mass_in = refs[:3]
        refs = refs[3:]
    if last:
        own_out, other_out, bias_ref = refs
    else:
        acc_out, peak_out, mass_out, bias_ref = refs
    seen = (seg_q[...] == seg_k[...]) & (pos_k[...] <= pos_q[...])
    bias_ref[...] = jnp.where(seen, 0.0, MASKED)
    rows = q_ref.shape[0]
    width = seg_k.shape[1]
    factor = math.log2(math.e) / math.sqrt(HD)
    heads = q_ref.shape[1] // HD
    cols = [slice(head * HD, (head + 1) * HD) for head in range(heads)]
    pairs = {}

    def key_values(head):
        which = head // group
        if which not in pairs:
            keys = jnp.concatenate([block[which, 0] for block in blocks], axis=0)
            values = jnp.concatenate([block[which, 1] for block in blocks], axis=0)
            pairs[which] = keys, jnp.concatenate([values, jnp.ones_like(values)], axis=1)
        return pairs[which]

    def score(head):
        keys = key_values(head)[0]
        scores = lax.dot_general(
            q_ref[:, cols[head]], keys, (((1,), (1,)), ((), ())), preferred_element_type=jnp.float32
        )
        return scores + bias_ref[...]

    def weigh(head, scores):
        peak = jnp.broadcast_to(jnp.max(scores, axis=1, keepdims=True), (rows, HD))
        if not first:
            peak = jnp.maximum(peak, peak_in[:, cols[head]])
        shift = peak * factor
        weights = [
            jnp.exp2(scores[:, at : at + HD] * factor - shift).astype(jnp.bfloat16)
            for at in range(0, width, HD)
        ]
        return peak, jnp.concatenate(weights, axis=1)

    def add_up(head, peak, weights):
        total = jnp.dot(weights, key_values(head)[1], preferred_element_type=jnp.float32)
        acc = total[:, :HD]
        mass = total[:, HD:]
        if not first:
            keep = jnp.exp2((peak_in[:, cols[head]] - peak) * factor)
            acc = acc + acc_in[:, cols[head]] * keep
            mass = mass + mass_in[:, cols[head]] * keep
        if last:
            result = (acc / mass).astype(jnp.bfloat16)
            own_out[:, cols[head]] = result[: rows // 2]
            other_out[:, cols[head]] = result[rows // 2 :]
        else:
            acc_out[:, cols[head]] = acc
            peak_out[:, cols[head]] = peak
            mass_out[:, cols[head]] = mass

    if last:
        for start in range(0, heads, 4):
            many = range(start, start + 4)
            scores = [score(head) for head in many]
            weighed = [weigh(head, scores[head - start]) for head in many]
            for head in many:
                add_up(head, *weighed[head - start])
    else:
        ahead = score(0)
        for head in range(heads):
            scores, ahead = ahead, score(head + 1) if head + 1 < heads else None
            add_up(head, *weigh(head, scores))


def attend(query, query_labels, blocks, key_labels, group, state, last):
    rows, q_cols = query.shape
    seg_k, pos_k = (jnp.concatenate(parts)[None, :] for parts in zip(*key_labels))
    seg_q, pos_q = (part[:, None] for part in query_labels)
    keys = len(blocks) * rows
    args = [seg_q, pos_q, seg_k, pos_k, query]
    args += [block.block if isinstance(block, Farthest) else block for block in blocks]
    first = state is None
    args += [] if first else state
    if last:
        outs = [jax.ShapeDtypeStruct((rows // 2, q_cols), jnp.bfloat16)] * 2
    else:
        outs = [jax.ShapeDtypeStruct((rows, q_cols), jnp.float32)] * 3
    return call(
        functools.partial(attention_kernel, len(blocks), first, last, group),
        "attend",
        args,
        outs,
        6 * rows * keys * q_cols,
        limit=14,
        scratch=[pltpu.VMEM((rows, keys), jnp.float32)],
        exps=rows * keys * q_cols // HD,
    )


def project_out_kernel(x_ref, w_ref, out_ref):
    tile = 512
    for start in range(0, out_ref.shape[1], tile):
        cols = slice(start, start + tile)
        part = jnp.dot(x_ref[...], w_ref[:, cols], preferred_element_type=jnp.float32)
        out_ref[:, cols] = part.astype(out_ref.dtype)


def project_out(rows, w_out, kind):
    out = jax.ShapeDtypeStruct((rows.shape[0], w_out.shape[1]), kind)
    flops = 2 * rows.shape[0] * w_out.size
    return call(project_out_kernel, "project_out", (rows, w_out), out, flops)


def finish_kernel(parts, tokens_ref, *refs):
    mixed_hbm, out_hbm, mixed, out, sems = refs[2 * parts :]
    copies = []
    first = 0
    for part in range(parts):
        mine, theirs = refs[2 * part : 2 * part + 2]
        tile = 1024
        for start in range(0, mine.shape[1], tile):
            cols = slice(start, start + tile)
            at = slice(first + start, first + start + tile)
            branch = mine[:, cols] + theirs[:, cols].astype(jnp.float32)
            out[:, at] = branch.astype(out.dtype)
            mixed[:, at] = (tokens_ref[:, at].astype(jnp.float32) + branch).astype(mixed.dtype)
            for here, there in ((out, out_hbm), (mixed, mixed_hbm)):
                sem = sems.at[len(copies)]
                copies.append(pltpu.make_async_copy(here.at[:, at], there.at[:, at], sem))
                copies[-1].start()
        first += mine.shape[1]
    for copy in copies:
        copy.wait()


def finish(tokens, parts):
    args = [tokens] + [array for part in parts for array in part]
    return call(
        functools.partial(finish_kernel, len(parts)),
        "finish",
        args,
        [jax.ShapeDtypeStruct(tokens.shape, jnp.bfloat16)] * 2,
        2 * tokens.size,
        scratch=[
            pltpu.VMEM(tokens.shape, jnp.bfloat16),
            pltpu.VMEM(tokens.shape, jnp.bfloat16),
            pltpu.SemaphoreType.DMA((tokens.shape[1] // 512,)),
        ],
        out_specs=IN_PLACE,
    )


def after(values, *others):
    return lax.optimization_barrier((values, others))[0]


def swap_cores(value):
    return lax.ppermute(value, "kv", [(0, 1), (1, 0)])


class Farthest(typing.NamedTuple):
    block: jax.Array
    first: jax.Array


def cube_exchanges(block, index, core, count):
    half = count // 2
    rows = block.shape[2]
    page = rows // 2

    def exchange(value, bit):
        return lax.ppermute(value, "seq", [(i, i ^ bit) for i in range(count)])

    from_x, from_y, from_z = exchange(block, 1), exchange(block, 2), exchange(block, 4)
    work = yield [(from_x, index ^ 1), (from_y, index ^ 2), (from_z, index ^ 4)]
    from_y = after(from_y, work)
    from_xy = exchange(from_y, 1)
    from_x = after(from_x, from_y)
    from_xz = exchange(from_x, 4)
    from_z = after(from_z, from_x)
    from_yz = exchange(from_z, 2)
    work = yield [(from_xy, index ^ 3), (from_yz, index ^ 6), (from_xz, index ^ 5)]
    from_xy, from_yz, from_xz = (after(value, work) for value in (from_xy, from_yz, from_xz))
    seam_page = lax.dynamic_slice_in_dim(from_xy, (1 - core) * page, page, 2)
    up = jnp.where(
        index % half == half // 2,
        seam_page.reshape(-1, HD),
        from_xy[2:].reshape(-1, HD),
    )
    swapped = {}
    for low in range(half // 2, count, half):
        swapped[low] = (low + half // 2) % count
    pairs = [(i, swapped.get(i, i ^ 4)) for i in range(count)]
    part_x, part_y = exchange(from_yz[:1], 1), exchange(from_xz[1:2], 2)
    part_z = lax.ppermute(up, "seq", pairs)
    first = index % half == 0
    usual = jnp.concatenate([part_x, part_y, part_z.reshape(2, 2, rows, HD)])
    before = part_z.reshape(4, 2, page, HD)
    before = jnp.concatenate([before, before], axis=2)
    yield [(Farthest(jnp.where(first, before, usual), first), index ^ 7)]


def distance_exchanges(block, index, count, reach):
    step = 3
    for start in range(1, reach + 1, step):
        received = []
        for distance in range(start, min(start + step, reach + 1)):
            moved = lax.ppermute(block, "seq", [(i, i + distance) for i in range(count - distance)])
            received.append((moved, index - distance))
        work = yield received
        block = after(block, work)


def shards(tokens, gain, w_query, w_key, w_value, w_out, segment_ids, page_table):
    half_rows = tokens.shape[0]
    block_rows = 2 * half_rows
    count = lax.axis_size("seq")
    index = lax.axis_index("seq")
    core = lax.axis_index("kv")
    reach = min(8, count // 2 - 1)

    other_tokens = swap_cores(tokens)
    normed, staged_gain, staged_key, staged_value = stage(tokens, gain, w_key, w_value)
    other_normed, own_block = project_kv(
        normed, other_tokens, staged_gain, staged_key, staged_value
    )
    page_table, index, core = after((page_table, index, core), own_block)

    if count == 2 * (reach + 1) and count // 2 == 8:
        exchanges = cube_exchanges(own_block, index, core, count)
    else:
        exchanges = distance_exchanges(own_block, index, count, reach)
    group = [(own_block, index)] + next(exchanges)

    query = project_query(normed, other_normed, w_query)

    offsets = jnp.arange(half_rows, dtype=jnp.int32)
    local = jnp.concatenate([core * half_rows + offsets, (1 - core) * half_rows + offsets])

    def labels(source):
        starts = (core * half_rows, (1 - core) * half_rows)
        begin = jnp.maximum(source, 0) * block_rows
        found = [lax.dynamic_slice_in_dim(segment_ids, begin + s, half_rows) for s in starts]
        return jnp.where(source >= 0, jnp.concatenate(found), -1), source * block_rows + local

    def labels_before():
        begin = index * block_rows - half_rows
        found = lax.dynamic_slice_in_dim(segment_ids, jnp.maximum(begin, 0), half_rows)
        nothing = jnp.full((half_rows,), -1, jnp.int32)
        segs = jnp.concatenate([jnp.where(index > 0, found, -1), nothing])
        return segs, jnp.concatenate([begin + offsets, begin + offsets])

    def key_labels(block, source):
        if not isinstance(block, Farthest):
            return labels(source)
        return jax.tree.map(
            lambda before, usual: jnp.where(block.first, before, usual),
            labels_before(),
            labels(source),
        )

    heads = own_block.shape[0]
    pages = own_block.reshape(heads, 2, 2, half_rows, HD).transpose(2, 1, 0, 3, 4)
    own_slot = lax.dynamic_index_in_dim(page_table, core, keepdims=False)
    page_pool = jnp.where(own_slot == 0, pages, pages[::-1])

    groups = query.shape[1] // HD // heads
    state, done = None, query
    while group:
        blocks = [block for block, _ in group]
        keys = [key_labels(block, source) for block, source in group]
        try:
            following = exchanges.send(done)
        except StopIteration:
            following = None
        state = attend(
            query, labels(index), blocks, keys, groups, state, following is None
        )
        group, done = following, (state, page_pool)
    attention = state

    own_rows, other_rows = attention
    theirs = project_out(other_rows, w_out, jnp.bfloat16)
    mine = project_out(after(own_rows, theirs), w_out, jnp.float32)
    mixed, attn_out = finish(tokens, [(mine, swap_cores(theirs))])
    return (mixed, attn_out, page_pool)


def solution(mesh):
    in_specs = (
        P(("seq", "kv"), None),
        P(),
        P(None, "kv"),
        P(None, "kv"),
        P(None, "kv"),
        P("kv", None),
        P(),
        P("seq"),
    )
    out_specs = (P(("seq", "kv"), None), P(("seq", "kv"), None), P("seq", None, "kv", None, None))
    return jax.shard_map(shards, mesh=mesh, in_specs=in_specs, out_specs=out_specs, check_vma=False)
```

```python
import functools
import math
import typing

import jax
import jax.numpy as jnp
from jax import lax
from jax.experimental import pallas as pl
from jax.experimental.pallas import tpu as pltpu
from jax.sharding import PartitionSpec as P

HD = 128
NORM_EPS = 1e-05
MASKED = -1e30
MIB = 1024 * 1024


IN_VMEM = pl.BlockSpec(memory_space=pltpu.VMEM)
IN_PLACE = pl.BlockSpec(memory_space=pltpu.HBM)


def call(
    kernel,
    name,
    args,
    outs,
    flops,
    limit=8,
    scratch=(),
    in_specs=None,
    out_specs=IN_VMEM,
    exps=0,
    aliases=None,
):
    outs_list = outs if isinstance(outs, list) else [outs]
    moved = sum(math.prod(a.shape) * a.dtype.itemsize for a in list(args) + outs_list)
    return pl.pallas_call(
        kernel,
        in_specs=in_specs or [IN_VMEM] * len(args),
        out_specs=jax.tree.map(lambda _: out_specs, outs),
        out_shape=outs,
        scratch_shapes=scratch,
        input_output_aliases=aliases or {},
        compiler_params=pltpu.CompilerParams(vmem_limit_bytes=limit * MIB),
        cost_estimate=pl.CostEstimate(flops=flops, bytes_accessed=moved, transcendentals=exps),
        name=name,
    )(
        *(
            pltpu.with_memory_space_constraint(arg, pltpu.HBM) if spec is IN_PLACE else arg
            for arg, spec in zip(args, in_specs or [IN_VMEM] * len(args))
        )
    )


def norm_rows(x_ref, gain_ref, out_ref):
    step = 16
    for start in range(0, x_ref.shape[0], step):
        wide = x_ref[start : start + step, :].astype(jnp.float32)
        mean = jnp.mean(wide * wide, axis=1, keepdims=True)
        normed = wide * lax.rsqrt(mean + NORM_EPS) * gain_ref[...]
        out_ref[start : start + step, :] = normed.astype(jnp.bfloat16)


def stream(copies, ahead, use):
    for n in range(min(ahead, len(copies))):
        for copy in copies[n]:
            copy.start()
    for n in range(len(copies)):
        for copy in copies[n]:
            copy.wait()
        if n + ahead < len(copies):
            for copy in copies[n + ahead]:
                copy.start()
        use(n)


def stage_kernel(
    tokens_hbm, gain_hbm, wk_hbm, wv_hbm, normed_ref, gain_ref, wk_ref, wv_ref, x_ref, sems
):
    pairs = ((tokens_hbm, x_ref), (gain_hbm, gain_ref), (wk_hbm, wk_ref), (wv_hbm, wv_ref))
    copies = [pltpu.make_async_copy(*pair, sems.at[n]) for n, pair in enumerate(pairs)]
    for copy in copies:
        copy.start()
    copies[0].wait()
    copies[1].wait()
    norm_rows(x_ref, gain_ref, normed_ref)
    copies[2].wait()
    copies[3].wait()


def stage(tokens, gain, w_key, w_value):
    gain = gain[None, :]
    return call(
        stage_kernel,
        "stage",
        (tokens, gain, w_key, w_value),
        [jax.ShapeDtypeStruct(a.shape, a.dtype) for a in (tokens, gain, w_key, w_value)],
        4 * tokens.size,
        scratch=[pltpu.VMEM(tokens.shape, tokens.dtype), pltpu.SemaphoreType.DMA((4,))],
        in_specs=[IN_PLACE] * 4,
    )


def project_kv_kernel(own_ref, other_ref, gain_ref, wk_ref, wv_ref, normed_ref, kv_ref):
    norm_rows(other_ref, gain_ref, normed_ref)
    rows = jnp.concatenate([own_ref[...], normed_ref[...]], axis=0)
    for head in range(kv_ref.shape[0]):
        cols = slice(head * HD, (head + 1) * HD)
        weights = jnp.concatenate([wk_ref[:, cols], wv_ref[:, cols]], axis=1)
        pair = jnp.dot(rows, weights, preferred_element_type=jnp.float32).astype(jnp.bfloat16)
        kv_ref[head, 0] = pair[:, :HD]
        kv_ref[head, 1] = pair[:, HD:]


def project_kv(normed, other_tokens, gain, w_key, w_value):
    half, width = normed.shape
    heads = w_key.shape[1] // HD
    outs = [
        jax.ShapeDtypeStruct((half, width), jnp.bfloat16),
        jax.ShapeDtypeStruct((heads, 2, 2 * half, HD), jnp.bfloat16),
    ]
    flops = 8 * half * width * heads * HD
    args = (normed, other_tokens, gain, w_key, w_value)
    return call(project_kv_kernel, "project_kv", args, outs, flops)


def project_query_kernel(depth, own_ref, other_ref, w_hbm, out_ref, w_ref, acc_ref, sems):
    chunks = w_ref.shape[0] // depth
    copies = []
    for n in range(chunks):
        rows = slice(n * depth, (n + 1) * depth)
        copies.append([pltpu.make_async_copy(w_hbm.at[rows], w_ref.at[rows], sems.at[n])])

    def use(n):
        rows = slice(n * depth, (n + 1) * depth)
        x = jnp.concatenate([own_ref[:, rows], other_ref[:, rows]], axis=0)
        tile = 512
        for start in range(0, out_ref.shape[1], tile):
            cols = slice(start, start + tile)
            part = jnp.dot(x, w_ref[rows, cols], preferred_element_type=jnp.float32)
            if n:
                part = part + acc_ref[:, cols]
            if n < chunks - 1:
                acc_ref[:, cols] = part
            else:
                out_ref[:, cols] = part.astype(out_ref.dtype)

    stream(copies, 3, use)


def project_query(own, other, w_query, depth=512):
    out = (2 * own.shape[0], w_query.shape[1])
    return call(
        functools.partial(project_query_kernel, depth),
        "project_query",
        (own, other, w_query),
        jax.ShapeDtypeStruct(out, jnp.bfloat16),
        4 * own.shape[0] * w_query.size,
        limit=22,
        scratch=[
            pltpu.VMEM(w_query.shape, w_query.dtype),
            pltpu.VMEM(out, jnp.float32),
            pltpu.SemaphoreType.DMA((w_query.shape[0] // depth,)),
        ],
        in_specs=[IN_VMEM, IN_VMEM, IN_PLACE],
    )


def attention_kernel(block_count, first, last, group, *refs):
    seg_q, pos_q, seg_k, pos_k, q_ref = refs[:5]
    blocks = refs[5 : 5 + block_count]
    refs = refs[5 + block_count :]
    if not first:
        acc_in, peak_in, mass_in = refs[:3]
        refs = refs[3:]
    if last:
        own_out, other_out, bias_ref = refs
    else:
        acc_out, peak_out, mass_out, bias_ref = refs
    seen = (seg_q[...] == seg_k[...]) & (pos_k[...] <= pos_q[...])
    bias_ref[...] = jnp.where(seen, 0.0, MASKED)
    rows = q_ref.shape[0]
    width = seg_k.shape[1]
    factor = math.log2(math.e) / math.sqrt(HD)
    heads = q_ref.shape[1] // HD
    cols = [slice(head * HD, (head + 1) * HD) for head in range(heads)]
    pairs = {}

    def key_values(head):
        which = head // group
        if which not in pairs:
            keys = jnp.concatenate([block[which, 0] for block in blocks], axis=0)
            values = jnp.concatenate([block[which, 1] for block in blocks], axis=0)
            pairs[which] = keys, jnp.concatenate([values, jnp.ones_like(values)], axis=1)
        return pairs[which]

    def score(head):
        keys = key_values(head)[0]
        scores = lax.dot_general(
            q_ref[:, cols[head]], keys, (((1,), (1,)), ((), ())), preferred_element_type=jnp.float32
        )
        return scores + bias_ref[...]

    def weigh(head, scores):
        peak = jnp.broadcast_to(jnp.max(scores, axis=1, keepdims=True), (rows, HD))
        if not first:
            peak = jnp.maximum(peak, peak_in[:, cols[head]])
        shift = peak * factor
        weights = [
            jnp.exp2(scores[:, at : at + HD] * factor - shift).astype(jnp.bfloat16)
            for at in range(0, width, HD)
        ]
        return peak, jnp.concatenate(weights, axis=1)

    def add_up(head, peak, weights):
        total = jnp.dot(weights, key_values(head)[1], preferred_element_type=jnp.float32)
        acc = total[:, :HD]
        mass = total[:, HD:]
        if not first:
            keep = jnp.exp2((peak_in[:, cols[head]] - peak) * factor)
            acc = acc + acc_in[:, cols[head]] * keep
            mass = mass + mass_in[:, cols[head]] * keep
        if last:
            result = (acc / mass).astype(jnp.bfloat16)
            own_out[:, cols[head]] = result[: rows // 2]
            other_out[:, cols[head]] = result[rows // 2 :]
        else:
            acc_out[:, cols[head]] = acc
            peak_out[:, cols[head]] = peak
            mass_out[:, cols[head]] = mass

    if last:
        for start in range(0, heads, 8):
            many = range(start, start + 8)
            scores = [score(head) for head in many]
            weighed = [weigh(head, scores[head - start]) for head in many]
            for head in many:
                add_up(head, *weighed[head - start])
    else:
        ahead = score(0)
        for head in range(heads):
            scores, ahead = ahead, score(head + 1) if head + 1 < heads else None
            add_up(head, *weigh(head, scores))


def attend(query, query_labels, blocks, key_labels, group, state, last):
    rows, q_cols = query.shape
    seg_k, pos_k = (jnp.concatenate(parts)[None, :] for parts in zip(*key_labels))
    seg_q, pos_q = (part[:, None] for part in query_labels)
    keys = len(blocks) * rows
    args = [seg_q, pos_q, seg_k, pos_k, query]
    args += [block.block if isinstance(block, Farthest) else block for block in blocks]
    first = state is None
    args += [] if first else state
    if last:
        outs = [jax.ShapeDtypeStruct((rows // 2, q_cols), jnp.bfloat16)] * 2
    else:
        outs = [jax.ShapeDtypeStruct((rows, q_cols), jnp.float32)] * 3
    return call(
        functools.partial(attention_kernel, len(blocks), first, last, group),
        "attend",
        args,
        outs,
        6 * rows * keys * q_cols,
        limit=14,
        scratch=[pltpu.VMEM((rows, keys), jnp.float32)],
        exps=rows * keys * q_cols // HD,
    )


def project_out_kernel(x_ref, w_ref, out_ref):
    tile = 512
    for start in range(0, out_ref.shape[1], tile):
        cols = slice(start, start + tile)
        part = jnp.dot(x_ref[...], w_ref[:, cols], preferred_element_type=jnp.float32)
        out_ref[:, cols] = part.astype(out_ref.dtype)


def project_out(rows, w_out, kind):
    out = jax.ShapeDtypeStruct((rows.shape[0], w_out.shape[1]), kind)
    flops = 2 * rows.shape[0] * w_out.size
    return call(project_out_kernel, "project_out", (rows, w_out), out, flops)


def finish_kernel(parts, tokens_ref, *refs):
    mixed_hbm, out_hbm, mixed, out, sems = refs[2 * parts :]
    copies = []
    first = 0
    for part in range(parts):
        mine, theirs = refs[2 * part : 2 * part + 2]
        tile = 1024
        for start in range(0, mine.shape[1], tile):
            cols = slice(start, start + tile)
            at = slice(first + start, first + start + tile)
            branch = mine[:, cols] + theirs[:, cols].astype(jnp.float32)
            out[:, at] = branch.astype(out.dtype)
            mixed[:, at] = (tokens_ref[:, at].astype(jnp.float32) + branch).astype(mixed.dtype)
            for here, there in ((out, out_hbm), (mixed, mixed_hbm)):
                sem = sems.at[len(copies)]
                copies.append(pltpu.make_async_copy(here.at[:, at], there.at[:, at], sem))
                copies[-1].start()
        first += mine.shape[1]
    for copy in copies:
        copy.wait()


def finish(tokens, parts):
    args = [tokens] + [array for part in parts for array in part]
    return call(
        functools.partial(finish_kernel, len(parts)),
        "finish",
        args,
        [jax.ShapeDtypeStruct(tokens.shape, jnp.bfloat16)] * 2,
        2 * tokens.size,
        scratch=[
            pltpu.VMEM(tokens.shape, jnp.bfloat16),
            pltpu.VMEM(tokens.shape, jnp.bfloat16),
            pltpu.SemaphoreType.DMA((tokens.shape[1] // 512,)),
        ],
        out_specs=IN_PLACE,
    )


def after(values, *others):
    return lax.optimization_barrier((values, others))[0]


def swap_cores(value):
    return lax.ppermute(value, "kv", [(0, 1), (1, 0)])


class Farthest(typing.NamedTuple):
    block: jax.Array
    first: jax.Array


def cube_exchanges(block, index, core, count):
    half = count // 2
    rows = block.shape[2]
    page = rows // 2

    def exchange(value, bit):
        return lax.ppermute(value, "seq", [(i, i ^ bit) for i in range(count)])

    from_x, from_y, from_z = exchange(block, 1), exchange(block, 2), exchange(block, 4)
    work = yield [(from_x, index ^ 1), (from_y, index ^ 2), (from_z, index ^ 4)]
    from_y = after(from_y, work)
    from_xy = exchange(from_y, 1)
    from_x = after(from_x, from_y)
    from_xz = exchange(from_x, 4)
    from_z = after(from_z, from_x)
    from_yz = exchange(from_z, 2)
    work = yield [(from_xy, index ^ 3), (from_yz, index ^ 6), (from_xz, index ^ 5)]
    from_xy, from_yz, from_xz = (after(value, work) for value in (from_xy, from_yz, from_xz))
    seam_page = lax.dynamic_slice_in_dim(from_xy, (1 - core) * page, page, 2)
    up = jnp.where(
        index % half == half // 2,
        seam_page.reshape(-1, HD),
        from_xy[2:].reshape(-1, HD),
    )
    swapped = {}
    for low in range(half // 2, count, half):
        swapped[low] = (low + half // 2) % count
    pairs = [(i, swapped.get(i, i ^ 4)) for i in range(count)]
    part_x, part_y = exchange(from_yz[:1], 1), exchange(from_xz[1:2], 2)
    part_z = lax.ppermute(up, "seq", pairs)
    first = index % half == 0
    usual = jnp.concatenate([part_x, part_y, part_z.reshape(2, 2, rows, HD)])
    before = part_z.reshape(4, 2, page, HD)
    before = jnp.concatenate([before, before], axis=2)
    yield [(Farthest(jnp.where(first, before, usual), first), index ^ 7)]


def distance_exchanges(block, index, count, reach):
    step = 3
    for start in range(1, reach + 1, step):
        received = []
        for distance in range(start, min(start + step, reach + 1)):
            moved = lax.ppermute(block, "seq", [(i, i + distance) for i in range(count - distance)])
            received.append((moved, index - distance))
        work = yield received
        block = after(block, work)


def shards(tokens, gain, w_query, w_key, w_value, w_out, segment_ids, page_table):
    half_rows = tokens.shape[0]
    block_rows = 2 * half_rows
    count = lax.axis_size("seq")
    index = lax.axis_index("seq")
    core = lax.axis_index("kv")
    reach = min(8, count // 2 - 1)

    other_tokens = swap_cores(tokens)
    normed, staged_gain, staged_key, staged_value = stage(tokens, gain, w_key, w_value)
    other_normed, own_block = project_kv(
        normed, other_tokens, staged_gain, staged_key, staged_value
    )
    page_table, index, core = after((page_table, index, core), own_block)

    if count == 2 * (reach + 1) and count // 2 == 8:
        exchanges = cube_exchanges(own_block, index, core, count)
    else:
        exchanges = distance_exchanges(own_block, index, count, reach)
    group = [(own_block, index)] + next(exchanges)

    query = project_query(normed, other_normed, w_query)

    offsets = jnp.arange(half_rows, dtype=jnp.int32)
    local = jnp.concatenate([core * half_rows + offsets, (1 - core) * half_rows + offsets])

    def labels(source):
        starts = (core * half_rows, (1 - core) * half_rows)
        begin = jnp.maximum(source, 0) * block_rows
        found = [lax.dynamic_slice_in_dim(segment_ids, begin + s, half_rows) for s in starts]
        return jnp.where(source >= 0, jnp.concatenate(found), -1), source * block_rows + local

    def labels_before():
        begin = index * block_rows - half_rows
        found = lax.dynamic_slice_in_dim(segment_ids, jnp.maximum(begin, 0), half_rows)
        nothing = jnp.full((half_rows,), -1, jnp.int32)
        segs = jnp.concatenate([jnp.where(index > 0, found, -1), nothing])
        return segs, jnp.concatenate([begin + offsets, begin + offsets])

    def key_labels(block, source):
        if not isinstance(block, Farthest):
            return labels(source)
        return jax.tree.map(
            lambda before, usual: jnp.where(block.first, before, usual),
            labels_before(),
            labels(source),
        )

    heads = own_block.shape[0]
    pages = own_block.reshape(heads, 2, 2, half_rows, HD).transpose(2, 1, 0, 3, 4)
    own_slot = lax.dynamic_index_in_dim(page_table, core, keepdims=False)
    page_pool = jnp.where(own_slot == 0, pages, pages[::-1])

    groups = query.shape[1] // HD // heads
    state, done = None, query
    while group:
        blocks = [block for block, _ in group]
        keys = [key_labels(block, source) for block, source in group]
        try:
            following = exchanges.send(done)
        except StopIteration:
            following = None
        state = attend(
            query, labels(index), blocks, keys, groups, state, following is None
        )
        group, done = following, (state, page_pool)
    attention = state

    own_rows, other_rows = attention
    theirs = project_out(other_rows, w_out, jnp.bfloat16)
    mine = project_out(after(own_rows, theirs), w_out, jnp.float32)
    mixed, attn_out = finish(tokens, [(mine, swap_cores(theirs))])
    return (mixed, attn_out, page_pool)


def solution(mesh):
    in_specs = (
        P(("seq", "kv"), None),
        P(),
        P(None, "kv"),
        P(None, "kv"),
        P(None, "kv"),
        P("kv", None),
        P(),
        P("seq"),
    )
    out_specs = (P(("seq", "kv"), None), P(("seq", "kv"), None), P("seq", None, "kv", None, None))
    return jax.shard_map(shards, mesh=mesh, in_specs=in_specs, out_specs=out_specs, check_vma=False)
```

```python
import functools
import math
import typing

import jax
import jax.numpy as jnp
from jax import lax
from jax.experimental import pallas as pl
from jax.experimental.pallas import tpu as pltpu
from jax.sharding import PartitionSpec as P

HD = 128
NORM_EPS = 1e-05
MASKED = -1e30
MIB = 1024 * 1024


IN_VMEM = pl.BlockSpec(memory_space=pltpu.VMEM)
IN_PLACE = pl.BlockSpec(memory_space=pltpu.HBM)


def call(
    kernel,
    name,
    args,
    outs,
    flops,
    limit=8,
    scratch=(),
    in_specs=None,
    out_specs=IN_VMEM,
    exps=0,
    aliases=None,
):
    outs_list = outs if isinstance(outs, list) else [outs]
    moved = sum(math.prod(a.shape) * a.dtype.itemsize for a in list(args) + outs_list)
    return pl.pallas_call(
        kernel,
        in_specs=in_specs or [IN_VMEM] * len(args),
        out_specs=jax.tree.map(lambda _: out_specs, outs),
        out_shape=outs,
        scratch_shapes=scratch,
        input_output_aliases=aliases or {},
        compiler_params=pltpu.CompilerParams(vmem_limit_bytes=limit * MIB),
        cost_estimate=pl.CostEstimate(flops=flops, bytes_accessed=moved, transcendentals=exps),
        name=name,
    )(
        *(
            pltpu.with_memory_space_constraint(arg, pltpu.HBM) if spec is IN_PLACE else arg
            for arg, spec in zip(args, in_specs or [IN_VMEM] * len(args))
        )
    )


def norm_rows(x_ref, gain_ref, out_ref):
    step = 16
    for start in range(0, x_ref.shape[0], step):
        wide = x_ref[start : start + step, :].astype(jnp.float32)
        mean = jnp.mean(wide * wide, axis=1, keepdims=True)
        normed = wide * lax.rsqrt(mean + NORM_EPS) * gain_ref[...]
        out_ref[start : start + step, :] = normed.astype(jnp.bfloat16)


def stream(copies, ahead, use):
    for n in range(min(ahead, len(copies))):
        for copy in copies[n]:
            copy.start()
    for n in range(len(copies)):
        for copy in copies[n]:
            copy.wait()
        if n + ahead < len(copies):
            for copy in copies[n + ahead]:
                copy.start()
        use(n)


def stage_kernel(
    tokens_hbm, gain_hbm, wk_hbm, wv_hbm, normed_ref, gain_ref, wk_ref, wv_ref, own_ref, x_ref, sems
):
    pairs = ((tokens_hbm, x_ref), (gain_hbm, gain_ref), (wk_hbm, wk_ref), (wv_hbm, wv_ref))
    copies = [pltpu.make_async_copy(*pair, sems.at[n]) for n, pair in enumerate(pairs)]
    for copy in copies:
        copy.start()
    copies[0].wait()
    copies[1].wait()
    norm_rows(x_ref, gain_ref, normed_ref)
    for which, ref in enumerate((wk_ref, wv_ref)):
        copies[2 + which].wait()
        part = jnp.dot(normed_ref[...], ref[...], preferred_element_type=jnp.float32)
        for head in range(own_ref.shape[0]):
            own_ref[head, which] = part[:, head * HD : (head + 1) * HD].astype(own_ref.dtype)


def stage(tokens, gain, w_key, w_value):
    gain = gain[None, :]
    return call(
        stage_kernel,
        "stage",
        (tokens, gain, w_key, w_value),
        [jax.ShapeDtypeStruct(a.shape, a.dtype) for a in (tokens, gain, w_key, w_value)]
        + [jax.ShapeDtypeStruct((w_key.shape[1] // HD, 2, tokens.shape[0], HD), jnp.bfloat16)],
        4 * tokens.size,
        scratch=[pltpu.VMEM(tokens.shape, tokens.dtype), pltpu.SemaphoreType.DMA((4,))],
        in_specs=[IN_PLACE] * 4,
    )


def project_kv_kernel(own_ref, other_ref, gain_ref, wk_ref, wv_ref, normed_ref, kv_ref):
    norm_rows(other_ref, gain_ref, normed_ref)
    half = other_ref.shape[0]
    kv_ref[:, :, :half] = own_ref[...]
    for head in range(kv_ref.shape[0]):
        cols = slice(head * HD, (head + 1) * HD)
        weights = jnp.concatenate([wk_ref[:, cols], wv_ref[:, cols]], axis=1)
        pair = jnp.dot(normed_ref[...], weights, preferred_element_type=jnp.float32)
        pair = pair.astype(jnp.bfloat16)
        kv_ref[head, 0, half:] = pair[:, :HD]
        kv_ref[head, 1, half:] = pair[:, HD:]


def project_kv(own_part, other_tokens, gain, w_key, w_value):
    half, width = other_tokens.shape
    heads = w_key.shape[1] // HD
    outs = [
        jax.ShapeDtypeStruct((half, width), jnp.bfloat16),
        jax.ShapeDtypeStruct((heads, 2, 2 * half, HD), jnp.bfloat16),
    ]
    flops = 8 * half * width * heads * HD
    args = (own_part, other_tokens, gain, w_key, w_value)
    return call(project_kv_kernel, "project_kv", args, outs, flops)


def project_query_kernel(depth, own_ref, other_ref, w_hbm, out_ref, w_ref, acc_ref, sems):
    chunks = w_ref.shape[0] // depth
    copies = []
    for n in range(chunks):
        rows = slice(n * depth, (n + 1) * depth)
        copies.append([pltpu.make_async_copy(w_hbm.at[rows], w_ref.at[rows], sems.at[n])])

    def use(n):
        rows = slice(n * depth, (n + 1) * depth)
        x = jnp.concatenate([own_ref[:, rows], other_ref[:, rows]], axis=0)
        tile = 512
        for start in range(0, out_ref.shape[1], tile):
            cols = slice(start, start + tile)
            part = jnp.dot(x, w_ref[rows, cols], preferred_element_type=jnp.float32)
            if n:
                part = part + acc_ref[:, cols]
            if n < chunks - 1:
                acc_ref[:, cols] = part
            else:
                out_ref[:, cols] = part.astype(out_ref.dtype)

    stream(copies, 3, use)


def project_query(own, other, w_query, depth=512):
    out = (2 * own.shape[0], w_query.shape[1])
    return call(
        functools.partial(project_query_kernel, depth),
        "project_query",
        (own, other, w_query),
        jax.ShapeDtypeStruct(out, jnp.bfloat16),
        4 * own.shape[0] * w_query.size,
        limit=22,
        scratch=[
            pltpu.VMEM(w_query.shape, w_query.dtype),
            pltpu.VMEM(out, jnp.float32),
            pltpu.SemaphoreType.DMA((w_query.shape[0] // depth,)),
        ],
        in_specs=[IN_VMEM, IN_VMEM, IN_PLACE],
    )


def attention_kernel(block_count, first, last, group, *refs):
    seg_q, pos_q, seg_k, pos_k, q_ref = refs[:5]
    blocks = refs[5 : 5 + block_count]
    refs = refs[5 + block_count :]
    if not first:
        acc_in, peak_in, mass_in = refs[:3]
        refs = refs[3:]
    if last:
        own_out, other_out, bias_ref = refs
    else:
        acc_out, peak_out, mass_out, bias_ref = refs
    seen = (seg_q[...] == seg_k[...]) & (pos_k[...] <= pos_q[...])
    bias_ref[...] = jnp.where(seen, 0.0, MASKED)
    rows = q_ref.shape[0]
    width = seg_k.shape[1]
    factor = math.log2(math.e) / math.sqrt(HD)
    heads = q_ref.shape[1] // HD
    cols = [slice(head * HD, (head + 1) * HD) for head in range(heads)]
    pairs = {}

    def key_values(head):
        which = head // group
        if which not in pairs:
            keys = jnp.concatenate([block[which, 0] for block in blocks], axis=0)
            values = jnp.concatenate([block[which, 1] for block in blocks], axis=0)
            pairs[which] = keys, jnp.concatenate([values, jnp.ones_like(values)], axis=1)
        return pairs[which]

    def score(head):
        keys = key_values(head)[0]
        scores = lax.dot_general(
            q_ref[:, cols[head]], keys, (((1,), (1,)), ((), ())), preferred_element_type=jnp.float32
        )
        return scores + bias_ref[...]

    def weigh(head, scores):
        peak = jnp.broadcast_to(jnp.max(scores, axis=1, keepdims=True), (rows, HD))
        if not first:
            peak = jnp.maximum(peak, peak_in[:, cols[head]])
        shift = peak * factor
        weights = [
            jnp.exp2(scores[:, at : at + HD] * factor - shift).astype(jnp.bfloat16)
            for at in range(0, width, HD)
        ]
        return peak, jnp.concatenate(weights, axis=1)

    def add_up(head, peak, weights):
        total = jnp.dot(weights, key_values(head)[1], preferred_element_type=jnp.float32)
        acc = total[:, :HD]
        mass = total[:, HD:]
        if not first:
            keep = jnp.exp2((peak_in[:, cols[head]] - peak) * factor)
            acc = acc + acc_in[:, cols[head]] * keep
            mass = mass + mass_in[:, cols[head]] * keep
        if last:
            result = (acc / mass).astype(jnp.bfloat16)
            own_out[:, cols[head]] = result[: rows // 2]
            other_out[:, cols[head]] = result[rows // 2 :]
        else:
            acc_out[:, cols[head]] = acc
            peak_out[:, cols[head]] = peak
            mass_out[:, cols[head]] = mass

    if last:
        for start in range(0, heads, 8):
            many = range(start, start + 8)
            scores = [score(head) for head in many]
            weighed = [weigh(head, scores[head - start]) for head in many]
            for head in many:
                add_up(head, *weighed[head - start])
    else:
        ahead = score(0)
        for head in range(heads):
            scores, ahead = ahead, score(head + 1) if head + 1 < heads else None
            add_up(head, *weigh(head, scores))


def attend(query, query_labels, blocks, key_labels, group, state, last):
    rows, q_cols = query.shape
    seg_k, pos_k = (jnp.concatenate(parts)[None, :] for parts in zip(*key_labels))
    seg_q, pos_q = (part[:, None] for part in query_labels)
    keys = len(blocks) * rows
    args = [seg_q, pos_q, seg_k, pos_k, query]
    args += [block.block if isinstance(block, Farthest) else block for block in blocks]
    first = state is None
    args += [] if first else state
    if last:
        outs = [jax.ShapeDtypeStruct((rows // 2, q_cols), jnp.bfloat16)] * 2
    else:
        outs = [jax.ShapeDtypeStruct((rows, q_cols), jnp.float32)] * 3
    return call(
        functools.partial(attention_kernel, len(blocks), first, last, group),
        "attend",
        args,
        outs,
        6 * rows * keys * q_cols,
        limit=14,
        scratch=[pltpu.VMEM((rows, keys), jnp.float32)],
        exps=rows * keys * q_cols // HD,
    )


def project_out_kernel(x_ref, w_ref, out_ref):
    tile = 512
    for start in range(0, out_ref.shape[1], tile):
        cols = slice(start, start + tile)
        part = jnp.dot(x_ref[...], w_ref[:, cols], preferred_element_type=jnp.float32)
        out_ref[:, cols] = part.astype(out_ref.dtype)


def project_out(rows, w_out, kind):
    out = jax.ShapeDtypeStruct((rows.shape[0], w_out.shape[1]), kind)
    flops = 2 * rows.shape[0] * w_out.size
    return call(project_out_kernel, "project_out", (rows, w_out), out, flops)


def finish_kernel(parts, tokens_ref, *refs):
    mixed_hbm, out_hbm, mixed, out, sems = refs[2 * parts :]
    copies = []
    first = 0
    for part in range(parts):
        mine, theirs = refs[2 * part : 2 * part + 2]
        tile = 1024
        for start in range(0, mine.shape[1], tile):
            cols = slice(start, start + tile)
            at = slice(first + start, first + start + tile)
            branch = mine[:, cols] + theirs[:, cols].astype(jnp.float32)
            out[:, at] = branch.astype(out.dtype)
            mixed[:, at] = (tokens_ref[:, at].astype(jnp.float32) + branch).astype(mixed.dtype)
            for here, there in ((out, out_hbm), (mixed, mixed_hbm)):
                sem = sems.at[len(copies)]
                copies.append(pltpu.make_async_copy(here.at[:, at], there.at[:, at], sem))
                copies[-1].start()
        first += mine.shape[1]
    for copy in copies:
        copy.wait()


def finish(tokens, parts):
    args = [tokens] + [array for part in parts for array in part]
    return call(
        functools.partial(finish_kernel, len(parts)),
        "finish",
        args,
        [jax.ShapeDtypeStruct(tokens.shape, jnp.bfloat16)] * 2,
        2 * tokens.size,
        scratch=[
            pltpu.VMEM(tokens.shape, jnp.bfloat16),
            pltpu.VMEM(tokens.shape, jnp.bfloat16),
            pltpu.SemaphoreType.DMA((tokens.shape[1] // 512,)),
        ],
        out_specs=IN_PLACE,
    )


def after(values, *others):
    return lax.optimization_barrier((values, others))[0]


def swap_cores(value):
    return lax.ppermute(value, "kv", [(0, 1), (1, 0)])


class Farthest(typing.NamedTuple):
    block: jax.Array
    first: jax.Array


def cube_exchanges(block, index, core, count):
    half = count // 2
    rows = block.shape[2]
    page = rows // 2

    def exchange(value, bit):
        return lax.ppermute(value, "seq", [(i, i ^ bit) for i in range(count)])

    from_x, from_y, from_z = exchange(block, 1), exchange(block, 2), exchange(block, 4)
    work = yield [(from_x, index ^ 1), (from_y, index ^ 2), (from_z, index ^ 4)]
    from_y = after(from_y, work)
    from_xy = exchange(from_y, 1)
    from_x = after(from_x, from_y)
    from_xz = exchange(from_x, 4)
    from_z = after(from_z, from_x)
    from_yz = exchange(from_z, 2)
    work = yield [(from_xy, index ^ 3), (from_yz, index ^ 6), (from_xz, index ^ 5)]
    from_xy, from_yz, from_xz = (after(value, work) for value in (from_xy, from_yz, from_xz))
    seam_page = lax.dynamic_slice_in_dim(from_xy, (1 - core) * page, page, 2)
    up = jnp.where(
        index % half == half // 2,
        seam_page.reshape(-1, HD),
        from_xy[2:].reshape(-1, HD),
    )
    swapped = {}
    for low in range(half // 2, count, half):
        swapped[low] = (low + half // 2) % count
    pairs = [(i, swapped.get(i, i ^ 4)) for i in range(count)]
    part_x, part_y = exchange(from_yz[:1], 1), exchange(from_xz[1:2], 2)
    part_z = lax.ppermute(up, "seq", pairs)
    first = index % half == 0
    usual = jnp.concatenate([part_x, part_y, part_z.reshape(2, 2, rows, HD)])
    before = part_z.reshape(4, 2, page, HD)
    before = jnp.concatenate([before, before], axis=2)
    yield [(Farthest(jnp.where(first, before, usual), first), index ^ 7)]


def distance_exchanges(block, index, count, reach):
    step = 3
    for start in range(1, reach + 1, step):
        received = []
        for distance in range(start, min(start + step, reach + 1)):
            moved = lax.ppermute(block, "seq", [(i, i + distance) for i in range(count - distance)])
            received.append((moved, index - distance))
        work = yield received
        block = after(block, work)


def shards(tokens, gain, w_query, w_key, w_value, w_out, segment_ids, page_table):
    half_rows = tokens.shape[0]
    block_rows = 2 * half_rows
    count = lax.axis_size("seq")
    index = lax.axis_index("seq")
    core = lax.axis_index("kv")
    reach = min(8, count // 2 - 1)

    other_tokens = swap_cores(tokens)
    normed, staged_gain, staged_key, staged_value, own_part = stage(tokens, gain, w_key, w_value)
    other_normed, own_block = project_kv(
        own_part, other_tokens, staged_gain, staged_key, staged_value
    )
    page_table, index, core = after((page_table, index, core), own_block)

    if count == 2 * (reach + 1) and count // 2 == 8:
        exchanges = cube_exchanges(own_block, index, core, count)
    else:
        exchanges = distance_exchanges(own_block, index, count, reach)
    group = [(own_block, index)] + next(exchanges)

    query = project_query(normed, other_normed, w_query)

    offsets = jnp.arange(half_rows, dtype=jnp.int32)
    local = jnp.concatenate([core * half_rows + offsets, (1 - core) * half_rows + offsets])

    def labels(source):
        starts = (core * half_rows, (1 - core) * half_rows)
        begin = jnp.maximum(source, 0) * block_rows
        found = [lax.dynamic_slice_in_dim(segment_ids, begin + s, half_rows) for s in starts]
        return jnp.where(source >= 0, jnp.concatenate(found), -1), source * block_rows + local

    def labels_before():
        begin = index * block_rows - half_rows
        found = lax.dynamic_slice_in_dim(segment_ids, jnp.maximum(begin, 0), half_rows)
        nothing = jnp.full((half_rows,), -1, jnp.int32)
        segs = jnp.concatenate([jnp.where(index > 0, found, -1), nothing])
        return segs, jnp.concatenate([begin + offsets, begin + offsets])

    def key_labels(block, source):
        if not isinstance(block, Farthest):
            return labels(source)
        return jax.tree.map(
            lambda before, usual: jnp.where(block.first, before, usual),
            labels_before(),
            labels(source),
        )

    heads = own_block.shape[0]
    pages = own_block.reshape(heads, 2, 2, half_rows, HD).transpose(2, 1, 0, 3, 4)
    own_slot = lax.dynamic_index_in_dim(page_table, core, keepdims=False)
    page_pool = jnp.where(own_slot == 0, pages, pages[::-1])

    groups = query.shape[1] // HD // heads
    state, done = None, query
    while group:
        blocks = [block for block, _ in group]
        keys = [key_labels(block, source) for block, source in group]
        try:
            following = exchanges.send(done)
        except StopIteration:
            following = None
        state = attend(
            query, labels(index), blocks, keys, groups, state, following is None
        )
        group, done = following, (state, page_pool)
    attention = state

    own_rows, other_rows = attention
    theirs = project_out(other_rows, w_out, jnp.bfloat16)
    mine = project_out(after(own_rows, theirs), w_out, jnp.float32)
    mixed, attn_out = finish(tokens, [(mine, swap_cores(theirs))])
    return (mixed, attn_out, page_pool)


def solution(mesh):
    in_specs = (
        P(("seq", "kv"), None),
        P(),
        P(None, "kv"),
        P(None, "kv"),
        P(None, "kv"),
        P("kv", None),
        P(),
        P("seq"),
    )
    out_specs = (P(("seq", "kv"), None), P(("seq", "kv"), None), P("seq", None, "kv", None, None))
    return jax.shard_map(shards, mesh=mesh, in_specs=in_specs, out_specs=out_specs, check_vma=False)
```

```python
import functools
import math
import typing

import jax
import jax.numpy as jnp
from jax import lax
from jax.experimental import pallas as pl
from jax.experimental.pallas import tpu as pltpu
from jax.sharding import PartitionSpec as P

HD = 128
NORM_EPS = 1e-05
MASKED = -1e30
MIB = 1024 * 1024


IN_VMEM = pl.BlockSpec(memory_space=pltpu.VMEM)
IN_PLACE = pl.BlockSpec(memory_space=pltpu.HBM)


def call(
    kernel,
    name,
    args,
    outs,
    flops,
    limit=8,
    scratch=(),
    in_specs=None,
    out_specs=IN_VMEM,
    exps=0,
    aliases=None,
):
    outs_list = outs if isinstance(outs, list) else [outs]
    moved = sum(math.prod(a.shape) * a.dtype.itemsize for a in list(args) + outs_list)
    return pl.pallas_call(
        kernel,
        in_specs=in_specs or [IN_VMEM] * len(args),
        out_specs=jax.tree.map(lambda _: out_specs, outs),
        out_shape=outs,
        scratch_shapes=scratch,
        input_output_aliases=aliases or {},
        compiler_params=pltpu.CompilerParams(vmem_limit_bytes=limit * MIB),
        cost_estimate=pl.CostEstimate(flops=flops, bytes_accessed=moved, transcendentals=exps),
        name=name,
    )(
        *(
            pltpu.with_memory_space_constraint(arg, pltpu.HBM) if spec is IN_PLACE else arg
            for arg, spec in zip(args, in_specs or [IN_VMEM] * len(args))
        )
    )


def norm_rows(x_ref, gain_ref, out_ref):
    step = 16
    for start in range(0, x_ref.shape[0], step):
        wide = x_ref[start : start + step, :].astype(jnp.float32)
        mean = jnp.mean(wide * wide, axis=1, keepdims=True)
        normed = wide * lax.rsqrt(mean + NORM_EPS) * gain_ref[...]
        out_ref[start : start + step, :] = normed.astype(jnp.bfloat16)


def stream(copies, ahead, use):
    for n in range(min(ahead, len(copies))):
        for copy in copies[n]:
            copy.start()
    for n in range(len(copies)):
        for copy in copies[n]:
            copy.wait()
        if n + ahead < len(copies):
            for copy in copies[n + ahead]:
                copy.start()
        use(n)


def stage_kernel(
    tokens_hbm, gain_hbm, wk_hbm, wv_hbm, normed_ref, gain_ref, wk_ref, wv_ref, own_ref, x_ref, sems
):
    pairs = ((tokens_hbm, x_ref), (gain_hbm, gain_ref), (wk_hbm, wk_ref), (wv_hbm, wv_ref))
    copies = [pltpu.make_async_copy(*pair, sems.at[n]) for n, pair in enumerate(pairs)]
    for copy in copies:
        copy.start()
    copies[0].wait()
    copies[1].wait()
    norm_rows(x_ref, gain_ref, normed_ref)
    for which, ref in enumerate((wk_ref, wv_ref)):
        copies[2 + which].wait()
        part = jnp.dot(normed_ref[...], ref[...], preferred_element_type=jnp.float32)
        for head in range(own_ref.shape[0]):
            own_ref[head, which] = part[:, head * HD : (head + 1) * HD].astype(own_ref.dtype)


def stage(tokens, gain, w_key, w_value):
    gain = gain[None, :]
    return call(
        stage_kernel,
        "stage",
        (tokens, gain, w_key, w_value),
        [jax.ShapeDtypeStruct(a.shape, a.dtype) for a in (tokens, gain, w_key, w_value)]
        + [jax.ShapeDtypeStruct((w_key.shape[1] // HD, 2, tokens.shape[0], HD), jnp.bfloat16)],
        4 * tokens.size,
        scratch=[pltpu.VMEM(tokens.shape, tokens.dtype), pltpu.SemaphoreType.DMA((4,))],
        in_specs=[IN_PLACE] * 4,
    )


def project_kv_kernel(own_ref, other_ref, gain_ref, wk_ref, wv_ref, normed_ref, kv_ref):
    norm_rows(other_ref, gain_ref, normed_ref)
    half = other_ref.shape[0]
    kv_ref[:, :, :half] = own_ref[...]
    for head in range(kv_ref.shape[0]):
        cols = slice(head * HD, (head + 1) * HD)
        weights = jnp.concatenate([wk_ref[:, cols], wv_ref[:, cols]], axis=1)
        pair = jnp.dot(normed_ref[...], weights, preferred_element_type=jnp.float32)
        pair = pair.astype(jnp.bfloat16)
        kv_ref[head, 0, half:] = pair[:, :HD]
        kv_ref[head, 1, half:] = pair[:, HD:]


def project_kv(own_part, other_tokens, gain, w_key, w_value):
    half, width = other_tokens.shape
    heads = w_key.shape[1] // HD
    outs = [
        jax.ShapeDtypeStruct((half, width), jnp.bfloat16),
        jax.ShapeDtypeStruct((heads, 2, 2 * half, HD), jnp.bfloat16),
    ]
    flops = 8 * half * width * heads * HD
    args = (own_part, other_tokens, gain, w_key, w_value)
    return call(project_kv_kernel, "project_kv", args, outs, flops)


def project_query_kernel(depth, own_ref, other_ref, w_hbm, out_ref, w_ref, acc_ref, sems):
    chunks = w_ref.shape[0] // depth
    copies = []
    for n in range(chunks):
        rows = slice(n * depth, (n + 1) * depth)
        copies.append([pltpu.make_async_copy(w_hbm.at[rows], w_ref.at[rows], sems.at[n])])

    def use(n):
        rows = slice(n * depth, (n + 1) * depth)
        x = jnp.concatenate([own_ref[:, rows], other_ref[:, rows]], axis=0)
        tile = 512
        for start in range(0, out_ref.shape[1], tile):
            cols = slice(start, start + tile)
            part = jnp.dot(x, w_ref[rows, cols], preferred_element_type=jnp.float32)
            if n:
                part = part + acc_ref[:, cols]
            if n < chunks - 1:
                acc_ref[:, cols] = part
            else:
                out_ref[:, cols] = part.astype(out_ref.dtype)

    stream(copies, 3, use)


def project_query(own, other, w_query, depth=512):
    out = (2 * own.shape[0], w_query.shape[1])
    return call(
        functools.partial(project_query_kernel, depth),
        "project_query",
        (own, other, w_query),
        jax.ShapeDtypeStruct(out, jnp.bfloat16),
        4 * own.shape[0] * w_query.size,
        limit=22,
        scratch=[
            pltpu.VMEM(w_query.shape, w_query.dtype),
            pltpu.VMEM(out, jnp.float32),
            pltpu.SemaphoreType.DMA((w_query.shape[0] // depth,)),
        ],
        in_specs=[IN_VMEM, IN_VMEM, IN_PLACE],
    )


def attention_kernel(block_count, first, last, group, *refs):
    seg_q, pos_q, seg_k, pos_k, q_ref = refs[:5]
    blocks = refs[5 : 5 + block_count]
    refs = refs[5 + block_count :]
    if not first:
        acc_in, peak_in, mass_in = refs[:3]
        refs = refs[3:]
    if last:
        own_out, other_out, bias_ref = refs
    else:
        acc_out, peak_out, mass_out, bias_ref = refs
    seen = (seg_q[...] == seg_k[...]) & (pos_k[...] <= pos_q[...])
    bias_ref[...] = jnp.where(seen, 0.0, MASKED)
    rows = q_ref.shape[0]
    width = seg_k.shape[1]
    factor = math.log2(math.e) / math.sqrt(HD)
    heads = q_ref.shape[1] // HD
    cols = [slice(head * HD, (head + 1) * HD) for head in range(heads)]
    pairs = {}

    def key_values(head):
        which = head // group
        if which not in pairs:
            keys = jnp.concatenate([block[which, 0] for block in blocks], axis=0)
            values = jnp.concatenate([block[which, 1] for block in blocks], axis=0)
            pairs[which] = keys, jnp.concatenate([values, jnp.ones_like(values)], axis=1)
        return pairs[which]

    def score(head):
        keys = key_values(head)[0]
        scores = lax.dot_general(
            q_ref[:, cols[head]], keys, (((1,), (1,)), ((), ())), preferred_element_type=jnp.float32
        )
        return scores + bias_ref[...]

    def weigh(head, scores):
        peak = jnp.broadcast_to(jnp.max(scores, axis=1, keepdims=True), (rows, HD))
        if not first:
            peak = jnp.maximum(peak, peak_in[:, cols[head]])
        shift = peak * factor
        weights = [
            jnp.exp2(scores[:, at : at + HD] * factor - shift).astype(jnp.bfloat16)
            for at in range(0, width, HD)
        ]
        return peak, jnp.concatenate(weights, axis=1)

    def add_up(head, peak, weights):
        total = jnp.dot(weights, key_values(head)[1], preferred_element_type=jnp.float32)
        acc = total[:, :HD]
        mass = total[:, HD:]
        if not first:
            keep = jnp.exp2((peak_in[:, cols[head]] - peak) * factor)
            acc = acc + acc_in[:, cols[head]] * keep
            mass = mass + mass_in[:, cols[head]] * keep
        if last:
            result = (acc / mass).astype(jnp.bfloat16)
            own_out[:, cols[head]] = result[: rows // 2]
            other_out[:, cols[head]] = result[rows // 2 :]
        else:
            acc_out[:, cols[head]] = acc
            peak_out[:, cols[head]] = peak
            mass_out[:, cols[head]] = mass

    if last:
        for start in range(0, heads, heads):
            many = range(start, start + heads)
            scores = [score(head) for head in many]
            weighed = [weigh(head, scores[head - start]) for head in many]
            for head in many:
                add_up(head, *weighed[head - start])
    else:
        ahead = score(0)
        for head in range(heads):
            scores, ahead = ahead, score(head + 1) if head + 1 < heads else None
            add_up(head, *weigh(head, scores))


def attend(query, query_labels, blocks, key_labels, group, state, last):
    rows, q_cols = query.shape
    seg_k, pos_k = (jnp.concatenate(parts)[None, :] for parts in zip(*key_labels))
    seg_q, pos_q = (part[:, None] for part in query_labels)
    keys = len(blocks) * rows
    args = [seg_q, pos_q, seg_k, pos_k, query]
    args += [block.block if isinstance(block, Farthest) else block for block in blocks]
    first = state is None
    args += [] if first else state
    if last:
        outs = [jax.ShapeDtypeStruct((rows // 2, q_cols), jnp.bfloat16)] * 2
    else:
        outs = [jax.ShapeDtypeStruct((rows, q_cols), jnp.float32)] * 3
    return call(
        functools.partial(attention_kernel, len(blocks), first, last, group),
        "attend",
        args,
        outs,
        6 * rows * keys * q_cols,
        limit=14,
        scratch=[pltpu.VMEM((rows, keys), jnp.float32)],
        exps=rows * keys * q_cols // HD,
    )


def project_out_kernel(x_ref, w_ref, out_ref):
    tile = 512
    for start in range(0, out_ref.shape[1], tile):
        cols = slice(start, start + tile)
        part = jnp.dot(x_ref[...], w_ref[:, cols], preferred_element_type=jnp.float32)
        out_ref[:, cols] = part.astype(out_ref.dtype)


def project_out(rows, w_out, kind):
    out = jax.ShapeDtypeStruct((rows.shape[0], w_out.shape[1]), kind)
    flops = 2 * rows.shape[0] * w_out.size
    return call(project_out_kernel, "project_out", (rows, w_out), out, flops)


def finish_kernel(parts, tokens_ref, *refs):
    mixed_hbm, out_hbm, mixed, out, sems = refs[2 * parts :]
    copies = []
    first = 0
    for part in range(parts):
        mine, theirs = refs[2 * part : 2 * part + 2]
        tile = 1024
        for start in range(0, mine.shape[1], tile):
            cols = slice(start, start + tile)
            at = slice(first + start, first + start + tile)
            branch = mine[:, cols] + theirs[:, cols].astype(jnp.float32)
            out[:, at] = branch.astype(out.dtype)
            mixed[:, at] = (tokens_ref[:, at].astype(jnp.float32) + branch).astype(mixed.dtype)
            for here, there in ((out, out_hbm), (mixed, mixed_hbm)):
                sem = sems.at[len(copies)]
                copies.append(pltpu.make_async_copy(here.at[:, at], there.at[:, at], sem))
                copies[-1].start()
        first += mine.shape[1]
    for copy in copies:
        copy.wait()


def finish(tokens, parts):
    args = [tokens] + [array for part in parts for array in part]
    return call(
        functools.partial(finish_kernel, len(parts)),
        "finish",
        args,
        [jax.ShapeDtypeStruct(tokens.shape, jnp.bfloat16)] * 2,
        2 * tokens.size,
        scratch=[
            pltpu.VMEM(tokens.shape, jnp.bfloat16),
            pltpu.VMEM(tokens.shape, jnp.bfloat16),
            pltpu.SemaphoreType.DMA((tokens.shape[1] // 512,)),
        ],
        out_specs=IN_PLACE,
    )


def after(values, *others):
    return lax.optimization_barrier((values, others))[0]


def swap_cores(value):
    return lax.ppermute(value, "kv", [(0, 1), (1, 0)])


class Farthest(typing.NamedTuple):
    block: jax.Array
    first: jax.Array


def cube_exchanges(block, index, core, count):
    half = count // 2
    rows = block.shape[2]
    page = rows // 2

    def exchange(value, bit):
        return lax.ppermute(value, "seq", [(i, i ^ bit) for i in range(count)])

    from_x, from_y, from_z = exchange(block, 1), exchange(block, 2), exchange(block, 4)
    work = yield [(from_x, index ^ 1), (from_y, index ^ 2), (from_z, index ^ 4)]
    from_y = after(from_y, work)
    from_xy = exchange(from_y, 1)
    from_x = after(from_x, from_y)
    from_xz = exchange(from_x, 4)
    from_z = after(from_z, from_x)
    from_yz = exchange(from_z, 2)
    work = yield [(from_xy, index ^ 3), (from_yz, index ^ 6), (from_xz, index ^ 5)]
    from_xy, from_yz, from_xz = (after(value, work) for value in (from_xy, from_yz, from_xz))
    seam_page = lax.dynamic_slice_in_dim(from_xy, (1 - core) * page, page, 2)
    up = jnp.where(
        index % half == half // 2,
        seam_page.reshape(-1, HD),
        from_xy[2:].reshape(-1, HD),
    )
    swapped = {}
    for low in range(half // 2, count, half):
        swapped[low] = (low + half // 2) % count
    pairs = [(i, swapped.get(i, i ^ 4)) for i in range(count)]
    part_x, part_y = exchange(from_yz[:1], 1), exchange(from_xz[1:2], 2)
    part_z = lax.ppermute(up, "seq", pairs)
    first = index % half == 0
    usual = jnp.concatenate([part_x, part_y, part_z.reshape(2, 2, rows, HD)])
    before = part_z.reshape(4, 2, page, HD)
    before = jnp.concatenate([before, before], axis=2)
    yield [(Farthest(jnp.where(first, before, usual), first), index ^ 7)]


def distance_exchanges(block, index, count, reach):
    step = 3
    for start in range(1, reach + 1, step):
        received = []
        for distance in range(start, min(start + step, reach + 1)):
            moved = lax.ppermute(block, "seq", [(i, i + distance) for i in range(count - distance)])
            received.append((moved, index - distance))
        work = yield received
        block = after(block, work)


def shards(tokens, gain, w_query, w_key, w_value, w_out, segment_ids, page_table):
    half_rows = tokens.shape[0]
    block_rows = 2 * half_rows
    count = lax.axis_size("seq")
    index = lax.axis_index("seq")
    core = lax.axis_index("kv")
    reach = min(8, count // 2 - 1)

    other_tokens = swap_cores(tokens)
    normed, staged_gain, staged_key, staged_value, own_part = stage(tokens, gain, w_key, w_value)
    other_normed, own_block = project_kv(
        own_part, other_tokens, staged_gain, staged_key, staged_value
    )
    page_table, index, core = after((page_table, index, core), own_block)

    if count == 2 * (reach + 1) and count // 2 == 8:
        exchanges = cube_exchanges(own_block, index, core, count)
    else:
        exchanges = distance_exchanges(own_block, index, count, reach)
    group = [(own_block, index)] + next(exchanges)

    query = project_query(normed, other_normed, w_query)

    offsets = jnp.arange(half_rows, dtype=jnp.int32)
    local = jnp.concatenate([core * half_rows + offsets, (1 - core) * half_rows + offsets])

    def labels(source):
        starts = (core * half_rows, (1 - core) * half_rows)
        begin = jnp.maximum(source, 0) * block_rows
        found = [lax.dynamic_slice_in_dim(segment_ids, begin + s, half_rows) for s in starts]
        return jnp.where(source >= 0, jnp.concatenate(found), -1), source * block_rows + local

    def labels_before():
        begin = index * block_rows - half_rows
        found = lax.dynamic_slice_in_dim(segment_ids, jnp.maximum(begin, 0), half_rows)
        nothing = jnp.full((half_rows,), -1, jnp.int32)
        segs = jnp.concatenate([jnp.where(index > 0, found, -1), nothing])
        return segs, jnp.concatenate([begin + offsets, begin + offsets])

    def key_labels(block, source):
        if not isinstance(block, Farthest):
            return labels(source)
        return jax.tree.map(
            lambda before, usual: jnp.where(block.first, before, usual),
            labels_before(),
            labels(source),
        )

    heads = own_block.shape[0]
    pages = own_block.reshape(heads, 2, 2, half_rows, HD).transpose(2, 1, 0, 3, 4)
    own_slot = lax.dynamic_index_in_dim(page_table, core, keepdims=False)
    page_pool = jnp.where(own_slot == 0, pages, pages[::-1])

    groups = query.shape[1] // HD // heads
    state, done = None, query
    while group:
        blocks = [block for block, _ in group]
        keys = [key_labels(block, source) for block, source in group]
        try:
            following = exchanges.send(done)
        except StopIteration:
            following = None
        state = attend(
            query, labels(index), blocks, keys, groups, state, following is None
        )
        group, done = following, (state, page_pool)
    attention = state

    own_rows, other_rows = attention
    theirs = project_out(other_rows, w_out, jnp.bfloat16)
    mine = project_out(after(own_rows, theirs), w_out, jnp.float32)
    mixed, attn_out = finish(tokens, [(mine, swap_cores(theirs))])
    return (mixed, attn_out, page_pool)


def solution(mesh):
    in_specs = (
        P(("seq", "kv"), None),
        P(),
        P(None, "kv"),
        P(None, "kv"),
        P(None, "kv"),
        P("kv", None),
        P(),
        P("seq"),
    )
    out_specs = (P(("seq", "kv"), None), P(("seq", "kv"), None), P("seq", None, "kv", None, None))
    return jax.shard_map(shards, mesh=mesh, in_specs=in_specs, out_specs=out_specs, check_vma=False)
```
